256 devices in a mesh: gx: 32 (over z, y), gy: 8 (over x, core).
Axes of the slice: x: 4, y: 4, z: 8, core: 2. Of those that a mesh axis runs over, the one named last changes fastest.
Arguments:
- flow_state: float32 [5, 256, 4, 1024], P(None, 'gx', None, 'gy'), may hold values from -1 to 4, as said below
Outputs:
- increment: float32 [5, 256, 4, 1024], P(None, 'gx', None, 'gy')
The draws below stay inside these ranges and needn't reach their ends.
Inputs may be any that keep to these rules, and one draw needn't show every extreme that they name: `flow_state`: density (component 0) lies between 0.6 and 1.4 and the pressure 0.4 (E - |m|^2 / (2 rho)) between 0.5 and 0.95 at every cell.
All inputs are finite; a program needn't handle non-finite values.
Results may differ from the reference program's by a relative error of at most 0.0003.
Values sent between devices are 32-bit elements; how exact they have to be, the bound alone decides.
No kernel may reach another device: no remote copies, remote signals or barrier semaphores. Data moves between devices by JAX's collectives and lax.ppermute only.
A program may use at most 256 MiB of HBM per device.

```python
import math
import jax
import jax.numpy as jnp
from jax import lax

NZ = 4
NX = 256
NY = 1024


def pattern_field(key, position_x, position_y):
    keys = jax.random.split(key, 3)
    waves_x = jax.random.randint(keys[0], (), 1, NX // 64 + 2).astype(jnp.float32)
    waves_y = jax.random.randint(keys[1], (), 1, NY // 64 + 2).astype(jnp.float32)
    phases = jax.random.uniform(keys[2], (2,), jnp.float32, 0.0, 2.0 * math.pi)
    return jnp.sin(2.0 * math.pi * waves_x * position_x / NX + phases[0]) * jnp.cos(2.0 * math.pi * waves_y * position_y / NY + phases[1])


def draw_flow_state(key, part):
    keys = jax.random.split(key, 12)
    position_x = jnp.arange(NX, dtype=jnp.float32)[:, None, None]
    position_z = jnp.arange(NZ, dtype=jnp.float32)[None, :, None]
    position_y = jnp.arange(NY, dtype=jnp.float32)[None, None, :]
    shape = (NX, NZ, NY)
    density_amp = 0.2
    pressure_amp = 0.15
    noises = [jax.random.uniform(keys[4 + i], shape, jnp.float32, -1.0, 1.0) for i in range(5)]
    phase_z = jax.random.uniform(keys[9], (), jnp.float32, 0.0, 2.0 * math.pi)
    density = (1.0 + density_amp * pattern_field(keys[0], position_x, position_y)) * (1.0 + 0.02 * noises[0])
    velocity_x = 0.5 + 0.25 * pattern_field(keys[1], position_x, position_y) + 0.02 * noises[1]
    velocity_y = 0.2 * pattern_field(keys[2], position_x, position_y) + 0.02 * noises[2]
    velocity_z = 0.1 * jnp.sin(2.0 * math.pi * position_z / NZ + phase_z) + 0.02 * noises[3]
    pressure = (1.0 + pressure_amp * pattern_field(keys[3], position_x, position_y)) / 1.4 * (1.0 + 0.02 * noises[4])
    density = jnp.broadcast_to(density, shape)
    velocity_x = jnp.broadcast_to(velocity_x, shape)
    velocity_y = jnp.broadcast_to(velocity_y, shape)
    velocity_z = jnp.broadcast_to(velocity_z, shape)
    energy = pressure / 0.4 + 0.5 * density * (velocity_x * velocity_x + velocity_y * velocity_y + velocity_z * velocity_z)
    return jnp.stack([density, density * velocity_x, density * velocity_y, density * velocity_z, energy]).astype(jnp.float32)


def setup_inputs(seed: int = 0) -> dict:
    streams_of = jax.random.split(jax.random.key(seed), 2)
    flow_state = draw_flow_state(jax.random.fold_in(streams_of[1], 71), 0)
    return dict(flow_state=flow_state)


HEAT_RATIO = 1.4
SPEED_RATIO = 20.0
IMPLICIT_DAMP = 1.0
EXPLICIT_DAMP = 0.05

def primitive(flow):
    density = flow[0]
    velocity_x = flow[1] / density
    velocity_y = flow[2] / density
    velocity_z = flow[3] / density
    kinetic = 0.5 * density * (velocity_x * velocity_x + velocity_y * velocity_y + velocity_z * velocity_z)
    pressure = (HEAT_RATIO - 1.0) * (flow[4] - kinetic)
    return (density, velocity_x, velocity_y, velocity_z, pressure)

def flux_along(flow, direction):
    density, velocity_x, velocity_y, velocity_z, pressure = primitive(flow)
    moving = (velocity_x, velocity_y, velocity_z)[direction]
    pieces = [flow[1 + direction], flow[1] * moving, flow[2] * moving, flow[3] * moving, (flow[4] + pressure) * moving]
    pieces[1 + direction] = pieces[1 + direction] + pressure
    return jnp.stack(pieces)

def jacobian_x(flow):
    density, velocity_x, velocity_y, velocity_z, pressure = primitive(flow)
    reduced_gamma = HEAT_RATIO - 1.0
    squared = velocity_x * velocity_x + velocity_y * velocity_y + velocity_z * velocity_z
    energy_term = 0.5 * reduced_gamma * squared
    enthalpy = (flow[4] + pressure) / density
    all_zeros = jnp.zeros_like(density)
    all_ones = jnp.ones_like(density)
    table = [[all_zeros, all_ones, all_zeros, all_zeros, all_zeros], [energy_term - velocity_x * velocity_x, (3.0 - HEAT_RATIO) * velocity_x, -reduced_gamma * velocity_y, -reduced_gamma * velocity_z, reduced_gamma * all_ones], [-velocity_x * velocity_y, velocity_y, velocity_x, all_zeros, all_zeros], [-velocity_x * velocity_z, velocity_z, all_zeros, velocity_x, all_zeros], [velocity_x * (energy_term - enthalpy), enthalpy - reduced_gamma * velocity_x * velocity_x, -reduced_gamma * velocity_x * velocity_y, -reduced_gamma * velocity_x * velocity_z, HEAT_RATIO * velocity_x]]
    return jnp.stack([jnp.stack(entries) for entries in table])

def explicit_residual(flow_state):
    along_x = flux_along(flow_state, 0)
    along_y = flux_along(flow_state, 1)
    along_z = flux_along(flow_state, 2)
    fourth_x = jnp.roll(flow_state, -2, axis=1) - 4.0 * jnp.roll(flow_state, -1, axis=1) + 6.0 * flow_state - 4.0 * jnp.roll(flow_state, 1, axis=1) + jnp.roll(flow_state, 2, axis=1)
    fourth_y = jnp.roll(flow_state, -2, axis=3) - 4.0 * jnp.roll(flow_state, -1, axis=3) + 6.0 * flow_state - 4.0 * jnp.roll(flow_state, 1, axis=3) + jnp.roll(flow_state, 2, axis=3)
    return -SPEED_RATIO * (jnp.roll(along_x, -1, axis=1) - jnp.roll(along_x, 1, axis=1)) - SPEED_RATIO * (jnp.roll(along_y, -1, axis=3) - jnp.roll(along_y, 1, axis=3)) - SPEED_RATIO * (jnp.roll(along_z, -1, axis=2) - jnp.roll(along_z, 1, axis=2)) - EXPLICIT_DAMP * (fourth_x + fourth_y)

def matmul_lines(former, latter):
    return jnp.einsum('zyij,zyjk->zyik', former, latter, precision=lax.Precision.HIGHEST)

def matvec_lines(former, latter):
    return jnp.einsum('zyij,zyj->zyi', former, latter, precision=lax.Precision.HIGHEST)

def reference(flow_state):
    residual = explicit_residual(flow_state)
    states = jnp.moveaxis(flow_state, 1, 0)
    sources = jnp.moveaxis(residual, 1, 0)
    prior_states = jnp.roll(states, 1, axis=0)
    next_states = jnp.roll(states, -1, axis=0)
    identity = jnp.eye(5, dtype=jnp.float32)
    depth = flow_state.shape[2]
    width = flow_state.shape[3]

    def forward(carried, inputs):
        former_coef, former_value = carried
        prior, ahead, source = inputs
        lower_band = -SPEED_RATIO * jnp.transpose(jacobian_x(prior), (2, 3, 0, 1)) - IMPLICIT_DAMP * identity
        upper_band = SPEED_RATIO * jnp.transpose(jacobian_x(ahead), (2, 3, 0, 1)) - IMPLICIT_DAMP * identity
        pivots = (1.0 + 2.0 * IMPLICIT_DAMP) * identity - matmul_lines(lower_band, former_coef)
        new_coef = jnp.linalg.solve(pivots, upper_band)
        moved = jnp.moveaxis(source, 0, -1) - matvec_lines(lower_band, former_value)
        new_value = jnp.linalg.solve(pivots, moved[..., None])[..., 0]
        return ((new_coef, new_value), (new_coef, new_value))
    start = (jnp.zeros((depth, width, 5, 5), jnp.float32), jnp.zeros((depth, width, 5), jnp.float32))
    _, (coefs, values) = lax.scan(forward, start, (prior_states, next_states, sources))

    def backward(ahead, inputs):
        coef, value = inputs
        result = value - matvec_lines(coef, ahead)
        return (result, result)
    _, solved = lax.scan(backward, jnp.zeros((depth, width, 5), jnp.float32), (coefs, values), reverse=True)
    return jnp.transpose(solved, (3, 0, 1, 2))
```

```python
import jax
import jax.numpy as jnp
from jax import lax
from jax.experimental import pallas as pl
from jax.experimental.pallas import tpu as pltpu
from jax.sharding import PartitionSpec as P

SPEED = 20.0
DAMP = 0.05
SCALE = SPEED / 3.0
SHARE = 1.0 / 3.0


def roll_lanes(value, amount):
    return value if amount % 128 == 0 else pltpu.roll(value, amount % 128, 1)


def roll_rows(value, amount):
    return value if amount % 8 == 0 else pltpu.roll(value, amount % 8, 0)


def lane_index():
    return lax.broadcasted_iota(jnp.int32, (8, 128), 1)


def row_index():
    return lax.broadcasted_iota(jnp.int32, (8, 128), 0)


def swap_bit(tiles, bit, width):
    shape = tiles[0].shape
    low = (lax.broadcasted_iota(jnp.int32, shape, 1) & width) == 0
    swapped = list(tiles)
    for i in range(len(tiles)):
        if not i & bit:
            first, second = tiles[i], tiles[i | bit]
            swapped[i] = jnp.where(low, first, roll_lanes(second, width))
            swapped[i | bit] = jnp.where(low, roll_lanes(first, -width), second)
    return swapped


def primitive(flow):
    inverse = 1.0 / flow[0]
    velocity = [flow[1] * inverse, flow[2] * inverse, flow[3] * inverse]
    squared = velocity[0] * velocity[0] + velocity[1] * velocity[1] + velocity[2] * velocity[2]
    pressure = 0.4 * (flow[4] - 0.5 * flow[0] * squared)
    return inverse, velocity, squared, pressure


def flux_along(flow, velocity, pressure, direction):
    moving = velocity[direction]
    pieces = [
        flow[1 + direction],
        flow[1] * moving,
        flow[2] * moving,
        flow[3] * moving,
        (flow[4] + pressure) * moving,
    ]
    pieces[1 + direction] = pieces[1 + direction] + pressure
    return pieces


def edge_kernel(flow_ref, edge_ref):
    lane = lane_index()
    packed = jnp.zeros((8, 128), jnp.float32)
    for v in range(20):
        tile = flow_ref[8 * v : 8 * v + 8, :]
        tail = (lane == 126 - 2 * v) | (lane == 127 - 2 * v)
        head = (lane == 2 * v) | (lane == 2 * v + 1)
        packed = jnp.where(tail, roll_lanes(tile, -2 * v), packed)
        packed = jnp.where(head, roll_lanes(tile, 2 * v), packed)
    edge_ref[...] = packed


def pack_kernel(flow_ref, left_ref, right_ref, out_ref):
    lane = lane_index()
    row = row_index()
    depth = row & 3
    left = left_ref[...]
    right = right_ref[...]
    both = [[None] * 8 for _ in range(5)]
    for xh in range(4):
        flow, edge = [], []
        for c in range(5):
            v = c * 4 + xh
            tile = flow_ref[8 * v : 8 * v + 8, :]
            flow.append(tile)
            beyond = jnp.where(lane < 2, roll_lanes(right, -2 * v), tile)
            edge.append(jnp.where(lane >= 126, roll_lanes(left, 2 * v), beyond))
        _, velocity, _, pressure = primitive(flow)
        along_y = flux_along(flow, velocity, pressure, 1)
        along_z = flux_along(flow, velocity, pressure, 2)
        _, edge_velocity, _, edge_pressure = primitive(edge)
        edge_y = flux_along(edge, edge_velocity, edge_pressure, 1)
        for c in range(5):
            q, e = flow[c], edge[c]
            minus_1 = roll_lanes(jnp.where(lane == 127, e, q), 1)
            minus_2 = roll_lanes(jnp.where(lane >= 126, e, q), 2)
            plus_1 = roll_lanes(jnp.where(lane == 0, e, q), -1)
            plus_2 = roll_lanes(jnp.where(lane < 2, e, q), -2)
            y_minus = roll_lanes(jnp.where(lane == 127, edge_y[c], along_y[c]), 1)
            y_plus = roll_lanes(jnp.where(lane == 0, edge_y[c], along_y[c]), -1)
            z = along_z[c]
            z_plus = jnp.where(depth == 3, roll_rows(z, 3), roll_rows(z, -1))
            z_minus = jnp.where(depth == 0, roll_rows(z, -3), roll_rows(z, 1))
            fourth = (plus_2 + minus_2) - 4.0 * (plus_1 + minus_1) + 6.0 * q
            partial = -SPEED * ((y_plus - y_minus) + (z_plus - z_minus)) - DAMP * fourth
            both[c][2 * xh] = jnp.where(row < 4, q, roll_rows(partial, 4))
            both[c][2 * xh + 1] = jnp.where(row < 4, roll_rows(q, 4), partial)
    for c in range(5):
        tiles = [both[c][(i & 1) * 4 + (i >> 2) * 2 + ((i >> 1) & 1)] for i in range(8)]
        tiles = swap_bit(tiles, 4, 64)
        tiles = swap_bit(tiles, 2, 32)
        tiles = swap_bit(tiles, 1, 16)
        for g in range(8):
            out_ref[pl.ds(g * 16 + c, 4, stride=128), :] = tiles[g][0:4]
            out_ref[pl.ds(g * 16 + 5 + c, 4, stride=128), :] = tiles[g][4:8]


def blocks_before(value, stride):
    if stride >= 8:
        return roll_rows(value, stride // 8)
    turned = roll_lanes(value, 16 * stride)
    return jnp.where(lane_index() < 16 * stride, roll_rows(turned, 1), turned)


def blocks_after(value, stride):
    if stride >= 8:
        return roll_rows(value, -(stride // 8))
    turned = roll_lanes(value, -16 * stride)
    return jnp.where(lane_index() >= 128 - 16 * stride, roll_rows(turned, -1), turned)


def jacobian_entries(flow):
    inverse, velocity, squared, pressure = primitive(flow)
    u, v, w = velocity
    f = 0.2 * squared
    h = (flow[4] + pressure) * inverse
    return [
        [None, 1.0, None, None, None],
        [f - u * u, 1.6 * u, -0.4 * v, -0.4 * w, 0.4],
        [-u * v, v, u, None, None],
        [-u * w, w, None, u, None],
        [u * (f - h), h - 0.4 * u * u, -0.4 * u * v, -0.4 * u * w, 1.4 * u],
    ], velocity, pressure


def scaled_plus(table, factor, shift):
    result = []
    for i in range(5):
        entries = []
        for j in range(5):
            entry = table[i][j]
            entry = None if entry is None else factor * entry
            if i == j:
                entry = shift if entry is None else entry + shift
            entries.append(entry)
        result.append(entries)
    return result


def kept_where(mask, table):
    return [[None if e is None else jnp.where(mask, e, 0.0) for e in row] for row in table]


def multiply(former, latter):
    columns = len(latter[0])
    result = []
    for i in range(5):
        entries = []
        for j in range(columns):
            total = None
            for k in range(5):
                if former[i][k] is None or latter[k][j] is None:
                    continue
                term = former[i][k] * latter[k][j]
                total = term if total is None else total + term
            entries.append(total)
        result.append(entries)
    return result


def add_tables(first, second):
    return [
        [b if a is None else (a if b is None else a + b) for a, b in zip(x, y)]
        for x, y in zip(first, second)
    ]


def identity_minus(table):
    return [[(1.0 - table[i][j]) if i == j else -table[i][j] for j in range(5)] for i in range(5)]


def dense(table):
    return [[e if hasattr(e, "shape") else jnp.full((8, 128), e, jnp.float32) for e in row] for row in table]


def solve(matrix, source):
    rows = [list(matrix[i]) + list(source[i]) for i in range(5)]
    width = len(rows[0])
    for k in range(5):
        if k < 4:
            largest = jnp.abs(rows[k][k])
            for j in range(k + 1, 5):
                candidate = jnp.abs(rows[j][k])
                better = candidate > largest
                largest = jnp.maximum(candidate, largest)
                for m in range(k, width):
                    upper, lower = rows[k][m], rows[j][m]
                    rows[k][m] = jnp.where(better, lower, upper)
                    rows[j][m] = jnp.where(better, upper, lower)
        inverse = 1.0 / rows[k][k]
        for m in range(k + 1, width):
            rows[k][m] = rows[k][m] * inverse
        for i in range(k + 1, 5):
            factor = rows[i][k]
            for m in range(k + 1, width):
                rows[i][m] = rows[i][m] - factor * rows[k][m]
    for k in range(4, 0, -1):
        for i in range(k):
            factor = rows[i][k]
            for m in range(5, width):
                rows[i][m] = rows[i][m] - factor * rows[k][m]
    return [rows[i][5:] for i in range(5)]


def side_by_side(*tables):
    return [sum((list(t[i]) for t in tables), []) for i in range(5)]


def columns_of(table, begin, end):
    return [row[begin:end] for row in table]


def mapped(function, table):
    return [[function(e) for e in row] for row in table]


def line_kernel(received_ref, out_ref):
    lane = lane_index()
    row = row_index()
    first_block = (row == 0) & (lane < 16)
    last_block = (row == 7) & (lane >= 112)

    def load(position):
        tiles = [received_ref[pl.ds(v * 16 + position, 8, stride=64), :] for v in range(4)]
        tiles = swap_bit(tiles, 2, 64)
        return swap_bit(tiles, 1, 32)

    flow = [load(c) for c in range(5)]
    partial = [load(5 + c) for c in range(5)]
    cells = {t: [flow[c][t] for c in range(5)] for t in range(4)}
    cells[-2] = [blocks_before(e, 1) for e in cells[2]]
    cells[-1] = [blocks_before(e, 1) for e in cells[3]]
    cells[4] = [blocks_after(e, 1) for e in cells[0]]
    cells[5] = [blocks_after(e, 1) for e in cells[1]]
    from_before, from_after, along_x = {}, {}, {}
    for t in range(-2, 5):
        table, velocity, pressure = jacobian_entries(cells[t])
        from_before[t] = scaled_plus(table, SCALE, SHARE)
        from_after[t] = scaled_plus(table, -SCALE, SHARE)
        along_x[t] = flux_along(cells[t], velocity, pressure, 0)
    from_before[-1] = kept_where(jnp.logical_not(first_block), from_before[-1])
    from_after[4] = kept_where(jnp.logical_not(last_block), from_after[4])
    right = {}
    for t in range(4):
        right[t] = []
        for c in range(5):
            fourth = (
                (cells[t + 2][c] + cells[t - 2][c])
                - 4.0 * (cells[t + 1][c] + cells[t - 1][c])
                + 6.0 * cells[t][c]
            )
            total = partial[c][t] - SPEED * (along_x[t + 1][c] - along_x[t - 1][c]) - DAMP * fourth
            right[t].append([total * SHARE])
    right[-1] = mapped(lambda e: blocks_before(e, 1), right[3])

    def eliminated(t):
        matrix = identity_minus(
            add_tables(
                multiply(from_after[t + 1], from_before[t]),
                multiply(from_before[t - 1], from_after[t]),
            )
        )
        before = dense(multiply(from_before[t - 1], from_before[t - 2]))
        after = dense(multiply(from_after[t + 1], from_after[t + 2]))
        value = add_tables(
            right[t],
            add_tables(
                multiply(from_after[t + 1], right[t + 1]), multiply(from_before[t - 1], right[t - 1])
            ),
        )
        return matrix, before, after, value

    def split(solved):
        return columns_of(solved, 0, 5), columns_of(solved, 5, 10), columns_of(solved, 10, 11)

    matrix, before, after, value = eliminated(2)
    half_before, half_after, half_value = split(solve(matrix, side_by_side(before, after, value)))
    matrix, before, after, value = eliminated(0)
    prior = lambda table: mapped(lambda e: blocks_before(e, 1), table)
    coupling = add_tables(multiply(after, half_before), multiply(before, prior(half_after)))
    matrix = [[m - c for m, c in zip(x, y)] for x, y in zip(matrix, coupling)]
    value = add_tables(
        value, add_tables(multiply(after, half_value), multiply(before, prior(half_value)))
    )
    before = multiply(before, prior(half_before))
    after = multiply(after, half_after)
    before, after, value = split(solve(matrix, side_by_side(before, after, value)))
    stride = 1
    while stride < 64:
        earlier = lambda table: mapped(lambda e: blocks_before(e, stride), table)
        later = lambda table: mapped(lambda e: blocks_after(e, stride), table)
        matrix = identity_minus(
            add_tables(multiply(before, earlier(after)), multiply(after, later(before)))
        )
        value = add_tables(
            value, add_tables(multiply(before, earlier(value)), multiply(after, later(value)))
        )
        if stride < 32:
            new_before = multiply(before, earlier(before))
            new_after = multiply(after, later(after))
            before, after, value = split(solve(matrix, side_by_side(new_before, new_after, value)))
        else:
            value = solve(matrix, value)
        stride *= 2
    result = {0: value}
    result[4] = mapped(lambda e: jnp.where(last_block, 0.0, blocks_after(e, 1)), value)
    result[2] = add_tables(
        half_value, add_tables(multiply(half_before, result[0]), multiply(half_after, result[4]))
    )
    for t in (1, 3):
        result[t] = add_tables(
            right[t],
            add_tables(
                multiply(from_before[t - 1], result[t - 1]), multiply(from_after[t + 1], result[t + 1])
            ),
        )
    for c in range(5):
        tiles = [result[t][c][0] for t in range(4)]
        tiles = swap_bit(tiles, 2, 64)
        tiles = swap_bit(tiles, 1, 32)
        for v in range(4):
            out_ref[pl.ds(v * 8 + c, 8, stride=32), :] = tiles[v]


def unpack_kernel(returned_ref, out_ref):
    for c in range(5):
        tiles = [returned_ref[pl.ds(g * 8 + c, 4, stride=64), :] for g in range(8)]
        tiles = swap_bit(tiles, 4, 64)
        tiles = swap_bit(tiles, 2, 32)
        tiles = swap_bit(tiles, 1, 16)
        for i in range(8):
            x = (i & 1) * 4 + (i >> 2) * 2 + ((i >> 1) & 1)
            out_ref[c * 32 + x * 4 : c * 32 + x * 4 + 4, :] = tiles[i]


def call(kernel, rows, *operands):
    whole = pl.BlockSpec(memory_space=pltpu.VMEM)
    return pl.pallas_call(
        kernel,
        out_shape=jax.ShapeDtypeStruct((rows, 128), jnp.float32),
        in_specs=[whole] * len(operands),
        out_specs=whole,
        compiler_params=pltpu.CompilerParams(vmem_limit_bytes=32 * 1024 * 1024),
    )(*operands)


def per_device(flow_state):
    flow = flow_state.reshape(160, 128)
    count = lax.axis_size("gy")
    edge = call(edge_kernel, 8, flow)
    left = lax.ppermute(edge, "gy", [(i, (i + 1) % count) for i in range(count)])
    right = lax.ppermute(edge, "gy", [((i + 1) % count, i) for i in range(count)])
    packed = call(pack_kernel, 512, flow, left, right)
    received = lax.all_to_all(
        packed.reshape(32, 16, 128), "gx", split_axis=0, concat_axis=0, tiled=True
    ).reshape(512, 128)
    solved = call(line_kernel, 256, received)
    returned = lax.all_to_all(
        solved.reshape(32, 8, 128), "gx", split_axis=0, concat_axis=0, tiled=True
    ).reshape(256, 128)
    return call(unpack_kernel, 160, returned).reshape(flow_state.shape)


def solution(mesh):
    placed = (P(None, "gx", None, "gy"),)
    return jax.shard_map(
        per_device, mesh=mesh, in_specs=placed, out_specs=P(None, "gx", None, "gy"), check_vma=False
    )
```

```python
import jax
import jax.numpy as jnp
from jax import lax
from jax.experimental import pallas as pl
from jax.experimental.pallas import tpu as pltpu
from jax.sharding import PartitionSpec as P

SPEED = 20.0
DAMP = 0.05
SCALE = SPEED / 3.0
SHARE = 1.0 / 3.0


def roll_lanes(value, amount):
    return value if amount % 128 == 0 else pltpu.roll(value, amount % 128, 1)


def roll_rows(value, amount):
    return value if amount % 8 == 0 else pltpu.roll(value, amount % 8, 0)


def lane_index():
    return lax.broadcasted_iota(jnp.int32, (8, 128), 1)


def row_index():
    return lax.broadcasted_iota(jnp.int32, (8, 128), 0)


def swap_bit(tiles, bit, width):
    shape = tiles[0].shape
    low = (lax.broadcasted_iota(jnp.int32, shape, 1) & width) == 0
    swapped = list(tiles)
    for i in range(len(tiles)):
        if not i & bit:
            first, second = tiles[i], tiles[i | bit]
            swapped[i] = jnp.where(low, first, roll_lanes(second, width))
            swapped[i | bit] = jnp.where(low, roll_lanes(first, -width), second)
    return swapped


def primitive(flow):
    inverse = 1.0 / flow[0]
    velocity = [flow[1] * inverse, flow[2] * inverse, flow[3] * inverse]
    squared = velocity[0] * velocity[0] + velocity[1] * velocity[1] + velocity[2] * velocity[2]
    pressure = 0.4 * (flow[4] - 0.5 * flow[0] * squared)
    return inverse, velocity, squared, pressure


def flux_along(flow, velocity, pressure, direction):
    moving = velocity[direction]
    pieces = [
        flow[1 + direction],
        flow[1] * moving,
        flow[2] * moving,
        flow[3] * moving,
        (flow[4] + pressure) * moving,
    ]
    pieces[1 + direction] = pieces[1 + direction] + pressure
    return pieces


def edge_kernel(flow_ref, edge_ref):
    lane = lane_index()
    packed = jnp.zeros((8, 128), jnp.float32)
    for v in range(20):
        tile = flow_ref[8 * v : 8 * v + 8, :]
        tail = (lane == 126 - 2 * v) | (lane == 127 - 2 * v)
        head = (lane == 2 * v) | (lane == 2 * v + 1)
        packed = jnp.where(tail, roll_lanes(tile, -2 * v), packed)
        packed = jnp.where(head, roll_lanes(tile, 2 * v), packed)
    edge_ref[...] = packed


def pack_kernel(flow_ref, left_ref, right_ref, out_ref):
    lane = lane_index()
    row = row_index()
    depth = row & 3
    left = left_ref[...]
    right = right_ref[...]
    both = [[None] * 8 for _ in range(5)]
    for xh in range(4):
        flow, edge = [], []
        for c in range(5):
            v = c * 4 + xh
            tile = flow_ref[8 * v : 8 * v + 8, :]
            flow.append(tile)
            beyond = jnp.where(lane < 2, roll_lanes(right, -2 * v), tile)
            edge.append(jnp.where(lane >= 126, roll_lanes(left, 2 * v), beyond))
        _, velocity, _, pressure = primitive(flow)
        along_y = flux_along(flow, velocity, pressure, 1)
        along_z = flux_along(flow, velocity, pressure, 2)
        _, edge_velocity, _, edge_pressure = primitive(edge)
        edge_y = flux_along(edge, edge_velocity, edge_pressure, 1)
        for c in range(5):
            q, e = flow[c], edge[c]
            minus_1 = roll_lanes(jnp.where(lane == 127, e, q), 1)
            minus_2 = roll_lanes(jnp.where(lane >= 126, e, q), 2)
            plus_1 = roll_lanes(jnp.where(lane == 0, e, q), -1)
            plus_2 = roll_lanes(jnp.where(lane < 2, e, q), -2)
            y_minus = roll_lanes(jnp.where(lane == 127, edge_y[c], along_y[c]), 1)
            y_plus = roll_lanes(jnp.where(lane == 0, edge_y[c], along_y[c]), -1)
            z = along_z[c]
            z_plus = jnp.where(depth == 3, roll_rows(z, 3), roll_rows(z, -1))
            z_minus = jnp.where(depth == 0, roll_rows(z, -3), roll_rows(z, 1))
            fourth = (plus_2 + minus_2) - 4.0 * (plus_1 + minus_1) + 6.0 * q
            partial = -SPEED * ((y_plus - y_minus) + (z_plus - z_minus)) - DAMP * fourth
            both[c][2 * xh] = jnp.where(row < 4, q, roll_rows(partial, 4))
            both[c][2 * xh + 1] = jnp.where(row < 4, roll_rows(q, 4), partial)
    for c in range(5):
        tiles = [both[c][(i & 1) * 4 + (i >> 2) * 2 + ((i >> 1) & 1)] for i in range(8)]
        tiles = swap_bit(tiles, 4, 64)
        tiles = swap_bit(tiles, 2, 32)
        tiles = swap_bit(tiles, 1, 16)
        for g in range(8):
            out_ref[pl.ds(g * 10 + c, 4, stride=80), :] = tiles[g][0:4]
            out_ref[pl.ds(g * 10 + 5 + c, 4, stride=80), :] = tiles[g][4:8]


def blocks_before(value, stride):
    if stride >= 8:
        return roll_rows(value, stride // 8)
    turned = roll_lanes(value, 16 * stride)
    return jnp.where(lane_index() < 16 * stride, roll_rows(turned, 1), turned)


def blocks_after(value, stride):
    if stride >= 8:
        return roll_rows(value, -(stride // 8))
    turned = roll_lanes(value, -16 * stride)
    return jnp.where(lane_index() >= 128 - 16 * stride, roll_rows(turned, -1), turned)


def jacobian_entries(flow):
    inverse, velocity, squared, pressure = primitive(flow)
    u, v, w = velocity
    f = 0.2 * squared
    h = (flow[4] + pressure) * inverse
    return [
        [None, 1.0, None, None, None],
        [f - u * u, 1.6 * u, -0.4 * v, -0.4 * w, 0.4],
        [-u * v, v, u, None, None],
        [-u * w, w, None, u, None],
        [u * (f - h), h - 0.4 * u * u, -0.4 * u * v, -0.4 * u * w, 1.4 * u],
    ], velocity, pressure


def scaled_plus(table, factor, shift):
    result = []
    for i in range(5):
        entries = []
        for j in range(5):
            entry = table[i][j]
            entry = None if entry is None else factor * entry
            if i == j:
                entry = shift if entry is None else entry + shift
            entries.append(entry)
        result.append(entries)
    return result


def kept_where(mask, table):
    return [[None if e is None else jnp.where(mask, e, 0.0) for e in row] for row in table]


def multiply(former, latter):
    columns = len(latter[0])
    result = []
    for i in range(5):
        entries = []
        for j in range(columns):
            total = None
            for k in range(5):
                if former[i][k] is None or latter[k][j] is None:
                    continue
                term = former[i][k] * latter[k][j]
                total = term if total is None else total + term
            entries.append(total)
        result.append(entries)
    return result


def add_tables(first, second):
    return [
        [b if a is None else (a if b is None else a + b) for a, b in zip(x, y)]
        for x, y in zip(first, second)
    ]


def identity_minus(table):
    return [[(1.0 - table[i][j]) if i == j else -table[i][j] for j in range(5)] for i in range(5)]


def dense(table):
    return [[e if hasattr(e, "shape") else jnp.full((8, 128), e, jnp.float32) for e in row] for row in table]


def solve(matrix, source):
    rows = [list(matrix[i]) + list(source[i]) for i in range(5)]
    width = len(rows[0])
    for k in range(5):
        if k < 4:
            largest = jnp.abs(rows[k][k])
            for j in range(k + 1, 5):
                candidate = jnp.abs(rows[j][k])
                better = candidate > largest
                largest = jnp.maximum(candidate, largest)
                for m in range(k, width):
                    upper, lower = rows[k][m], rows[j][m]
                    rows[k][m] = jnp.where(better, lower, upper)
                    rows[j][m] = jnp.where(better, upper, lower)
        inverse = 1.0 / rows[k][k]
        for m in range(k + 1, width):
            rows[k][m] = rows[k][m] * inverse
        for i in range(k + 1, 5):
            factor = rows[i][k]
            for m in range(k + 1, width):
                rows[i][m] = rows[i][m] - factor * rows[k][m]
    for k in range(4, 0, -1):
        for i in range(k):
            factor = rows[i][k]
            for m in range(5, width):
                rows[i][m] = rows[i][m] - factor * rows[k][m]
    return [rows[i][5:] for i in range(5)]


def side_by_side(*tables):
    return [sum((list(t[i]) for t in tables), []) for i in range(5)]


def columns_of(table, begin, end):
    return [row[begin:end] for row in table]


def mapped(function, table):
    return [[function(e) for e in row] for row in table]


def line_kernel(received_ref, out_ref):
    lane = lane_index()
    row = row_index()
    first_block = (row == 0) & (lane < 16)
    last_block = (row == 7) & (lane >= 112)

    def load(position):
        tiles = [received_ref[pl.ds(v * 10 + position, 8, stride=40), :] for v in range(4)]
        tiles = swap_bit(tiles, 2, 64)
        return swap_bit(tiles, 1, 32)

    flow = [load(c) for c in range(5)]
    partial = [load(5 + c) for c in range(5)]
    cells = {t: [flow[c][t] for c in range(5)] for t in range(4)}
    cells[-2] = [blocks_before(e, 1) for e in cells[2]]
    cells[-1] = [blocks_before(e, 1) for e in cells[3]]
    cells[4] = [blocks_after(e, 1) for e in cells[0]]
    cells[5] = [blocks_after(e, 1) for e in cells[1]]
    from_before, from_after, along_x = {}, {}, {}
    for t in range(-2, 5):
        table, velocity, pressure = jacobian_entries(cells[t])
        from_before[t] = scaled_plus(table, SCALE, SHARE)
        from_after[t] = scaled_plus(table, -SCALE, SHARE)
        along_x[t] = flux_along(cells[t], velocity, pressure, 0)
    from_before[-1] = kept_where(jnp.logical_not(first_block), from_before[-1])
    from_after[4] = kept_where(jnp.logical_not(last_block), from_after[4])
    right = {}
    for t in range(4):
        right[t] = []
        for c in range(5):
            fourth = (
                (cells[t + 2][c] + cells[t - 2][c])
                - 4.0 * (cells[t + 1][c] + cells[t - 1][c])
                + 6.0 * cells[t][c]
            )
            total = partial[c][t] - SPEED * (along_x[t + 1][c] - along_x[t - 1][c]) - DAMP * fourth
            right[t].append([total * SHARE])
    right[-1] = mapped(lambda e: blocks_before(e, 1), right[3])

    def eliminated(t):
        matrix = identity_minus(
            add_tables(
                multiply(from_after[t + 1], from_before[t]),
                multiply(from_before[t - 1], from_after[t]),
            )
        )
        before = dense(multiply(from_before[t - 1], from_before[t - 2]))
        after = dense(multiply(from_after[t + 1], from_after[t + 2]))
        value = add_tables(
            right[t],
            add_tables(
                multiply(from_after[t + 1], right[t + 1]), multiply(from_before[t - 1], right[t - 1])
            ),
        )
        return matrix, before, after, value

    def split(solved):
        return columns_of(solved, 0, 5), columns_of(solved, 5, 10), columns_of(solved, 10, 11)

    matrix, before, after, value = eliminated(2)
    half_before, half_after, half_value = split(solve(matrix, side_by_side(before, after, value)))
    matrix, before, after, value = eliminated(0)
    prior = lambda table: mapped(lambda e: blocks_before(e, 1), table)
    coupling = add_tables(multiply(after, half_before), multiply(before, prior(half_after)))
    matrix = [[m - c for m, c in zip(x, y)] for x, y in zip(matrix, coupling)]
    value = add_tables(
        value, add_tables(multiply(after, half_value), multiply(before, prior(half_value)))
    )
    before = multiply(before, prior(half_before))
    after = multiply(after, half_after)
    before, after, value = split(solve(matrix, side_by_side(before, after, value)))
    stride = 1
    while stride < 64:
        earlier = lambda table: mapped(lambda e: blocks_before(e, stride), table)
        later = lambda table: mapped(lambda e: blocks_after(e, stride), table)
        matrix = identity_minus(
            add_tables(multiply(before, earlier(after)), multiply(after, later(before)))
        )
        value = add_tables(
            value, add_tables(multiply(before, earlier(value)), multiply(after, later(value)))
        )
        if stride < 32:
            new_before = multiply(before, earlier(before))
            new_after = multiply(after, later(after))
            before, after, value = split(solve(matrix, side_by_side(new_before, new_after, value)))
        else:
            value = solve(matrix, value)
        stride *= 2
    result = {0: value}
    result[4] = mapped(lambda e: jnp.where(last_block, 0.0, blocks_after(e, 1)), value)
    result[2] = add_tables(
        half_value, add_tables(multiply(half_before, result[0]), multiply(half_after, result[4]))
    )
    for t in (1, 3):
        result[t] = add_tables(
            right[t],
            add_tables(
                multiply(from_before[t - 1], result[t - 1]), multiply(from_after[t + 1], result[t + 1])
            ),
        )
    for c in range(5):
        tiles = [result[t][c][0] for t in range(4)]
        tiles = swap_bit(tiles, 2, 64)
        tiles = swap_bit(tiles, 1, 32)
        for v in range(4):
            out_ref[pl.ds(v * 5 + c, 8, stride=20), :] = tiles[v]


def unpack_kernel(returned_ref, out_ref):
    for c in range(5):
        tiles = [returned_ref[pl.ds(g * 5 + c, 4, stride=40), :] for g in range(8)]
        tiles = swap_bit(tiles, 4, 64)
        tiles = swap_bit(tiles, 2, 32)
        tiles = swap_bit(tiles, 1, 16)
        for i in range(8):
            x = (i & 1) * 4 + (i >> 2) * 2 + ((i >> 1) & 1)
            out_ref[c * 32 + x * 4 : c * 32 + x * 4 + 4, :] = tiles[i]


def call(kernel, rows, *operands):
    whole = pl.BlockSpec(memory_space=pltpu.VMEM)
    return pl.pallas_call(
        kernel,
        out_shape=jax.ShapeDtypeStruct((rows, 128), jnp.float32),
        in_specs=[whole] * len(operands),
        out_specs=whole,
        compiler_params=pltpu.CompilerParams(vmem_limit_bytes=32 * 1024 * 1024),
    )(*operands)


def per_device(flow_state):
    flow = flow_state.reshape(160, 128)
    count = lax.axis_size("gy")
    edge = call(edge_kernel, 8, flow)
    left = lax.ppermute(edge, "gy", [(i, (i + 1) % count) for i in range(count)])
    right = lax.ppermute(edge, "gy", [((i + 1) % count, i) for i in range(count)])
    packed = call(pack_kernel, 320, flow, left, right)
    received = lax.all_to_all(
        packed.reshape(32, 1, 1280), "gx", split_axis=0, concat_axis=0, tiled=True
    ).reshape(320, 128)
    solved = call(line_kernel, 160, received)
    returned = lax.all_to_all(
        solved.reshape(32, 1, 640), "gx", split_axis=0, concat_axis=0, tiled=True
    ).reshape(160, 128)
    return call(unpack_kernel, 160, returned).reshape(flow_state.shape)


def solution(mesh):
    placed = (P(None, "gx", None, "gy"),)
    return jax.shard_map(
        per_device, mesh=mesh, in_specs=placed, out_specs=P(None, "gx", None, "gy"), check_vma=False
    )
```

```python
import jax
import jax.numpy as jnp
from jax import lax
from jax.experimental import pallas as pl
from jax.experimental.pallas import tpu as pltpu
from jax.sharding import PartitionSpec as P

SPEED = 20.0
DAMP = 0.05
SCALE = SPEED / 3.0
SHARE = 1.0 / 3.0


def roll_lanes(value, amount):
    return value if amount % 128 == 0 else pltpu.roll(value, amount % 128, 1)


def roll_rows(value, amount):
    return value if amount % 8 == 0 else pltpu.roll(value, amount % 8, 0)


def lane_index():
    return lax.broadcasted_iota(jnp.int32, (8, 128), 1)


def row_index():
    return lax.broadcasted_iota(jnp.int32, (8, 128), 0)


def swap_bit(tiles, bit, width):
    shape = tiles[0].shape
    low = (lax.broadcasted_iota(jnp.int32, shape, 1) & width) == 0
    swapped = list(tiles)
    for i in range(len(tiles)):
        if not i & bit:
            first, second = tiles[i], tiles[i | bit]
            swapped[i] = jnp.where(low, first, roll_lanes(second, width))
            swapped[i | bit] = jnp.where(low, roll_lanes(first, -width), second)
    return swapped


def primitive(flow):
    inverse = 1.0 / flow[0]
    velocity = [flow[1] * inverse, flow[2] * inverse, flow[3] * inverse]
    squared = velocity[0] * velocity[0] + velocity[1] * velocity[1] + velocity[2] * velocity[2]
    pressure = 0.4 * (flow[4] - 0.5 * flow[0] * squared)
    return inverse, velocity, squared, pressure


def flux_along(flow, velocity, pressure, direction):
    moving = velocity[direction]
    pieces = [
        flow[1 + direction],
        flow[1] * moving,
        flow[2] * moving,
        flow[3] * moving,
        (flow[4] + pressure) * moving,
    ]
    pieces[1 + direction] = pieces[1 + direction] + pressure
    return pieces


def edge_kernel(flow_ref, edge_ref):
    lane = lane_index()
    packed = jnp.zeros((8, 128), jnp.float32)
    for v in range(20):
        tile = flow_ref[8 * v : 8 * v + 8, :]
        tail = (lane == 126 - 2 * v) | (lane == 127 - 2 * v)
        head = (lane == 2 * v) | (lane == 2 * v + 1)
        packed = jnp.where(tail, roll_lanes(tile, -2 * v), packed)
        packed = jnp.where(head, roll_lanes(tile, 2 * v), packed)
    edge_ref[...] = packed


def pack_kernel(flow_ref, left_ref, right_ref, out_ref):
    lane = lane_index()
    row = row_index()
    depth = row & 3
    left = left_ref[...]
    right = right_ref[...]
    both = [[None] * 8 for _ in range(5)]
    for xh in range(4):
        flow, edge = [], []
        for c in range(5):
            v = c * 4 + xh
            tile = flow_ref[8 * v : 8 * v + 8, :]
            flow.append(tile)
            beyond = jnp.where(lane < 2, roll_lanes(right, -2 * v), tile)
            edge.append(jnp.where(lane >= 126, roll_lanes(left, 2 * v), beyond))
        _, velocity, _, pressure = primitive(flow)
        along_y = flux_along(flow, velocity, pressure, 1)
        along_z = flux_along(flow, velocity, pressure, 2)
        _, edge_velocity, _, edge_pressure = primitive(edge)
        edge_y = flux_along(edge, edge_velocity, edge_pressure, 1)
        for c in range(5):
            q, e = flow[c], edge[c]
            minus_1 = roll_lanes(jnp.where(lane == 127, e, q), 1)
            minus_2 = roll_lanes(jnp.where(lane >= 126, e, q), 2)
            plus_1 = roll_lanes(jnp.where(lane == 0, e, q), -1)
            plus_2 = roll_lanes(jnp.where(lane < 2, e, q), -2)
            y_minus = roll_lanes(jnp.where(lane == 127, edge_y[c], along_y[c]), 1)
            y_plus = roll_lanes(jnp.where(lane == 0, edge_y[c], along_y[c]), -1)
            z = along_z[c]
            z_plus = jnp.where(depth == 3, roll_rows(z, 3), roll_rows(z, -1))
            z_minus = jnp.where(depth == 0, roll_rows(z, -3), roll_rows(z, 1))
            fourth = (plus_2 + minus_2) - 4.0 * (plus_1 + minus_1) + 6.0 * q
            partial = -SPEED * ((y_plus - y_minus) + (z_plus - z_minus)) - DAMP * fourth
            both[c][2 * xh] = jnp.where(row < 4, q, roll_rows(partial, 4))
            both[c][2 * xh + 1] = jnp.where(row < 4, roll_rows(q, 4), partial)
    for c in range(5):
        tiles = both[c]
        tiles = swap_bit(tiles, 4, 64)
        tiles = swap_bit(tiles, 2, 32)
        tiles = swap_bit(tiles, 1, 16)
        for g in range(8):
            out_ref[pl.ds(g * 10 + c, 4, stride=80), :] = tiles[g][0:4]
            out_ref[pl.ds(g * 10 + 5 + c, 4, stride=80), :] = tiles[g][4:8]


def swapped_halves(value):
    return roll_rows(value, 4)


def in_top(top, bottom):
    return jnp.where(row_index() < 4, top, bottom)


def half_before(value, periodic=False):
    turned = roll_lanes(value, 16)
    carried = roll_rows(turned, 5)
    if periodic:
        carried = jnp.where(row_index() == 0, roll_rows(turned, 1), carried)
    earlier = jnp.where(lane_index() < 16, carried, roll_rows(turned, 4))
    return in_top(earlier, roll_rows(value, 4))


def half_after(value, periodic=False):
    turned = roll_lanes(value, -16)
    carried = roll_rows(turned, 3)
    if periodic:
        carried = jnp.where(row_index() == 7, roll_rows(turned, 7), carried)
    later = jnp.where(lane_index() >= 112, carried, roll_rows(turned, 4))
    return in_top(roll_rows(value, 4), later)


def blocks_before(value, stride):
    if stride >= 8:
        return roll_rows(value, stride // 8)
    turned = roll_lanes(value, 16 * stride)
    return jnp.where(lane_index() < 16 * stride, roll_rows(turned, 1), turned)


def blocks_after(value, stride):
    if stride >= 8:
        return roll_rows(value, -(stride // 8))
    turned = roll_lanes(value, -16 * stride)
    return jnp.where(lane_index() >= 128 - 16 * stride, roll_rows(turned, -1), turned)


def jacobian_entries(flow):
    inverse, velocity, squared, pressure = primitive(flow)
    u, v, w = velocity
    f = 0.2 * squared
    h = (flow[4] + pressure) * inverse
    return [
        [None, 1.0, None, None, None],
        [f - u * u, 1.6 * u, -0.4 * v, -0.4 * w, 0.4],
        [-u * v, v, u, None, None],
        [-u * w, w, None, u, None],
        [u * (f - h), h - 0.4 * u * u, -0.4 * u * v, -0.4 * u * w, 1.4 * u],
    ], velocity, pressure


def scaled_plus(table, factor, shift):
    result = []
    for i in range(5):
        entries = []
        for j in range(5):
            entry = table[i][j]
            entry = None if entry is None else factor * entry
            if i == j:
                entry = shift if entry is None else entry + shift
            entries.append(entry)
        result.append(entries)
    return result


def kept_where(mask, table):
    return [[None if e is None else jnp.where(mask, e, 0.0) for e in row] for row in table]


def multiply(former, latter):
    columns = len(latter[0])
    result = []
    for i in range(5):
        entries = []
        for j in range(columns):
            total = None
            for k in range(5):
                if former[i][k] is None or latter[k][j] is None:
                    continue
                term = former[i][k] * latter[k][j]
                total = term if total is None else total + term
            entries.append(total)
        result.append(entries)
    return result


def add_tables(first, second):
    return [
        [b if a is None else (a if b is None else a + b) for a, b in zip(x, y)]
        for x, y in zip(first, second)
    ]


def identity_minus(table):
    return [[(1.0 - table[i][j]) if i == j else -table[i][j] for j in range(5)] for i in range(5)]


def dense(table):
    return [[e if hasattr(e, "shape") else jnp.full((8, 128), e, jnp.float32) for e in row] for row in table]


def solve(matrix, source):
    rows = [list(matrix[i]) + list(source[i]) for i in range(5)]
    width = len(rows[0])
    for k in range(5):
        if k < 4:
            largest = jnp.abs(rows[k][k])
            for j in range(k + 1, 5):
                candidate = jnp.abs(rows[j][k])
                better = candidate > largest
                largest = jnp.maximum(candidate, largest)
                for m in range(k, width):
                    upper, lower = rows[k][m], rows[j][m]
                    rows[k][m] = jnp.where(better, lower, upper)
                    rows[j][m] = jnp.where(better, upper, lower)
        inverse = 1.0 / rows[k][k]
        for m in range(k + 1, width):
            rows[k][m] = rows[k][m] * inverse
        for i in range(k + 1, 5):
            factor = rows[i][k]
            for m in range(k + 1, width):
                rows[i][m] = rows[i][m] - factor * rows[k][m]
    for k in range(4, 0, -1):
        for i in range(k):
            factor = rows[i][k]
            for m in range(5, width):
                rows[i][m] = rows[i][m] - factor * rows[k][m]
    return [rows[i][5:] for i in range(5)]


def side_by_side(*tables):
    return [sum((list(t[i]) for t in tables), []) for i in range(5)]


def columns_of(table, begin, end):
    return [row[begin:end] for row in table]


def mapped(function, table):
    return [[function(e) for e in row] for row in table]


def both_halves(table):
    return mapped(lambda e: e + swapped_halves(e), table)


def minus(first, second):
    return [[a - b for a, b in zip(x, y)] for x, y in zip(first, second)]


def line_kernel(received_ref, out_ref):
    lane = lane_index()
    row = row_index()
    first_half = (row == 0) & (lane < 16)
    last_half = (row == 7) & (lane >= 112)
    straight = (row >= 4) == (lane >= 64)

    def exchanged(tile):
        return jnp.where(straight, tile, roll_lanes(swapped_halves(tile), 64))

    def load(position):
        tiles = []
        for u in range(4):
            halves = [
                received_ref[pl.ds((u + 4 * j) * 10 + position, 4, stride=80), :] for j in range(2)
            ]
            tiles.append(exchanged(jnp.concatenate(halves, axis=0)))
        return swap_bit(swap_bit(tiles, 2, 32), 1, 16)

    flow = [load(c) for c in range(5)]
    partial = [load(5 + c) for c in range(5)]
    cells = {t: [flow[c][t] for c in range(5)] for t in range(4)}
    cells[-2] = [half_before(e, True) for e in cells[2]]
    cells[-1] = [half_before(e, True) for e in cells[3]]
    cells[4] = [half_after(e, True) for e in cells[0]]
    cells[5] = [half_after(e, True) for e in cells[1]]
    from_before, from_after, along_x = {}, {}, {}
    for t in range(-2, 5):
        table, velocity, pressure = jacobian_entries(cells[t])
        from_before[t] = scaled_plus(table, SCALE, SHARE)
        from_after[t] = scaled_plus(table, -SCALE, SHARE)
        along_x[t] = flux_along(cells[t], velocity, pressure, 0)
    from_before[-1] = kept_where(jnp.logical_not(first_half), from_before[-1])
    from_after[4] = kept_where(jnp.logical_not(last_half), from_after[4])
    right = {}
    for t in range(4):
        right[t] = []
        for c in range(5):
            fourth = (
                (cells[t + 2][c] + cells[t - 2][c])
                - 4.0 * (cells[t + 1][c] + cells[t - 1][c])
                + 6.0 * cells[t][c]
            )
            total = partial[c][t] - SPEED * (along_x[t + 1][c] - along_x[t - 1][c]) - DAMP * fourth
            right[t].append([total * SHARE])
    right[-1] = mapped(half_before, right[3])

    def eliminated(t):
        matrix = identity_minus(
            add_tables(
                multiply(from_after[t + 1], from_before[t]),
                multiply(from_before[t - 1], from_after[t]),
            )
        )
        before = dense(multiply(from_before[t - 1], from_before[t - 2]))
        after = dense(multiply(from_after[t + 1], from_after[t + 2]))
        value = add_tables(
            right[t],
            add_tables(
                multiply(from_after[t + 1], right[t + 1]), multiply(from_before[t - 1], right[t - 1])
            ),
        )
        return matrix, before, after, value

    matrix, before, after, value = eliminated(2)
    solved = solve(matrix, side_by_side(before, after, value))
    fine_before, fine_after, fine_value = (
        columns_of(solved, 0, 5), columns_of(solved, 5, 10), columns_of(solved, 10, 11)
    )
    matrix, before, after, value = eliminated(0)
    matrix = minus(
        matrix,
        add_tables(
            multiply(after, fine_before), multiply(before, mapped(half_before, fine_after))
        ),
    )
    value = add_tables(
        value,
        add_tables(multiply(after, fine_value), multiply(before, mapped(half_before, fine_value))),
    )
    before = multiply(before, mapped(half_before, fine_before))
    after = multiply(after, fine_after)

    def pick(table, function):
        return mapped(lambda e: function(e, swapped_halves(e)), table)

    packed = [[in_top(a, swapped_halves(b)) for a, b in zip(x, y)] for x, y in zip(before, after)]
    second = [[in_top(swapped_halves(a), b) for a, b in zip(x, y)] for x, y in zip(before, after)]
    second_matrix = pick(matrix, lambda e, swapped: in_top(swapped, e))
    second_value = pick(value, lambda e, swapped: in_top(swapped, e))
    matrix = pick(matrix, in_top)
    value = pick(value, in_top)
    solved = solve(second_matrix, side_by_side(second, second_value))
    second, second_value = columns_of(solved, 0, 5), columns_of(solved, 5, 6)

    def top_before(table):
        return mapped(lambda e: in_top(blocks_before(e, 1), e), table)

    matrix = minus(matrix, both_halves(multiply(packed, mapped(half_before, second))))
    value = add_tables(value, both_halves(multiply(packed, top_before(second_value))))
    packed = multiply(packed, top_before(second))
    solved = solve(matrix, side_by_side(packed, value))
    packed, value = columns_of(solved, 0, 5), columns_of(solved, 5, 6)

    stride = 1
    while stride < 32:
        earlier = lambda table: mapped(lambda e: blocks_before(e, stride), table)
        later = lambda table: mapped(lambda e: blocks_after(e, stride), table)
        towards = lambda x, y: [[in_top(a, b) for a, b in zip(p, q)] for p, q in zip(x, y)]
        prior, following = earlier(packed), later(packed)
        crossed = mapped(swapped_halves, towards(following, prior))
        matrix = identity_minus(both_halves(multiply(packed, crossed)))
        beside = towards(earlier(value), later(value))
        value = add_tables(value, both_halves(multiply(packed, beside)))
        if stride < 16:
            packed = multiply(packed, towards(prior, following))
            solved = solve(matrix, side_by_side(packed, value))
            packed, value = columns_of(solved, 0, 5), columns_of(solved, 5, 6)
        else:
            value = solve(matrix, value)
        stride *= 2

    last_block = ((row & 3) == 3) & (lane >= 112)
    ahead = mapped(lambda e: jnp.where(last_block, 0.0, blocks_after(e, 1)), value)
    around = [[in_top(a[0], b[0])] for a, b in zip(value, ahead)]
    middle = add_tables(second_value, both_halves(multiply(second, around)))
    result = {
        0: [[in_top(a[0], b[0])] for a, b in zip(value, middle)],
        4: [[in_top(a[0], b[0])] for a, b in zip(middle, ahead)],
    }
    result[2] = add_tables(
        fine_value, add_tables(multiply(fine_before, result[0]), multiply(fine_after, result[4]))
    )
    for t in (1, 3):
        result[t] = add_tables(
            right[t],
            add_tables(
                multiply(from_before[t - 1], result[t - 1]), multiply(from_after[t + 1], result[t + 1])
            ),
        )
    for c in range(5):
        tiles = swap_bit(swap_bit([result[t][c][0] for t in range(4)], 2, 32), 1, 16)
        for u in range(4):
            tile = exchanged(tiles[u])
            for j in range(2):
                out_ref[pl.ds((u + 4 * j) * 5 + c, 4, stride=40), :] = tile[4 * j : 4 * j + 4]


def unpack_kernel(returned_ref, out_ref):
    for c in range(5):
        tiles = [returned_ref[pl.ds(g * 5 + c, 4, stride=40), :] for g in range(8)]
        tiles = swap_bit(tiles, 4, 64)
        tiles = swap_bit(tiles, 2, 32)
        tiles = swap_bit(tiles, 1, 16)
        for x in range(8):
            out_ref[c * 32 + x * 4 : c * 32 + x * 4 + 4, :] = tiles[x]


def call(kernel, rows, *operands):
    whole = pl.BlockSpec(memory_space=pltpu.VMEM)
    return pl.pallas_call(
        kernel,
        out_shape=jax.ShapeDtypeStruct((rows, 128), jnp.float32),
        in_specs=[whole] * len(operands),
        out_specs=whole,
        compiler_params=pltpu.CompilerParams(vmem_limit_bytes=32 * 1024 * 1024),
    )(*operands)


def per_device(flow_state):
    flow = flow_state.reshape(160, 128)
    count = lax.axis_size("gy")
    edge = call(edge_kernel, 8, flow)
    left = lax.ppermute(edge, "gy", [(i, (i + 1) % count) for i in range(count)])
    right = lax.ppermute(edge, "gy", [((i + 1) % count, i) for i in range(count)])
    packed = call(pack_kernel, 320, flow, left, right)
    received = lax.all_to_all(
        packed.reshape(32, 1, 1280), "gx", split_axis=0, concat_axis=0, tiled=True
    ).reshape(320, 128)
    solved = call(line_kernel, 160, received)
    returned = lax.all_to_all(
        solved.reshape(32, 1, 640), "gx", split_axis=0, concat_axis=0, tiled=True
    ).reshape(160, 128)
    return call(unpack_kernel, 160, returned).reshape(flow_state.shape)


def solution(mesh):
    placed = (P(None, "gx", None, "gy"),)
    return jax.shard_map(
        per_device, mesh=mesh, in_specs=placed, out_specs=P(None, "gx", None, "gy"), check_vma=False
    )
```

```python
import jax
import jax.numpy as jnp
from jax import lax
from jax.experimental import pallas as pl
from jax.experimental.pallas import tpu as pltpu
from jax.sharding import PartitionSpec as P

SPEED = 20.0
DAMP = 0.05
SCALE = SPEED / 3.0
SHARE = 1.0 / 3.0


def roll_lanes(value, amount):
    return value if amount % 128 == 0 else pltpu.roll(value, amount % 128, 1)


def roll_rows(value, amount):
    return value if amount % 8 == 0 else pltpu.roll(value, amount % 8, 0)


def lane_index():
    return lax.broadcasted_iota(jnp.int32, (8, 128), 1)


def row_index():
    return lax.broadcasted_iota(jnp.int32, (8, 128), 0)


def swap_bit(tiles, bit, width):
    shape = tiles[0].shape
    low = (lax.broadcasted_iota(jnp.int32, shape, 1) & width) == 0
    swapped = list(tiles)
    for i in range(len(tiles)):
        if not i & bit:
            first, second = tiles[i], tiles[i | bit]
            swapped[i] = jnp.where(low, first, roll_lanes(second, width))
            swapped[i | bit] = jnp.where(low, roll_lanes(first, -width), second)
    return swapped


def primitive(flow):
    inverse = 1.0 / flow[0]
    velocity = [flow[1] * inverse, flow[2] * inverse, flow[3] * inverse]
    squared = velocity[0] * velocity[0] + velocity[1] * velocity[1] + velocity[2] * velocity[2]
    pressure = 0.4 * (flow[4] - 0.5 * flow[0] * squared)
    return inverse, velocity, squared, pressure


def flux_along(flow, velocity, pressure, direction):
    moving = velocity[direction]
    pieces = [
        flow[1 + direction],
        flow[1] * moving,
        flow[2] * moving,
        flow[3] * moving,
        (flow[4] + pressure) * moving,
    ]
    pieces[1 + direction] = pieces[1 + direction] + pressure
    return pieces


def edge_kernel(flow_ref, edge_ref):
    lane = lane_index()
    top = row_index() < 4
    for c in range(5):
        packed = None
        for xh in range(4):
            v = c * 4 + xh
            tile = flow_ref[8 * v : 8 * v + 8, :]
            turned = roll_lanes(tile, 16)
            for xl in range(2):
                if xl == 0:
                    chosen = jnp.where(top, turned, roll_rows(tile, 4))
                else:
                    chosen = jnp.where(top, roll_rows(turned, 4), tile)
                x = 2 * xh + xl
                chosen = roll_lanes(chosen, 16 * x)
                packed = chosen if packed is None else jnp.where(lane >= 16 * x, chosen, packed)
        edge_ref[8 * c : 8 * c + 8, :] = packed


def pack_kernel(flow_ref, out_ref):
    lane = lane_index()
    row = row_index()
    depth = row & 3
    both = [[None] * 8 for _ in range(5)]
    for xh in range(4):
        flow = []
        for c in range(5):
            v = c * 4 + xh
            flow.append(flow_ref[8 * v : 8 * v + 8, :])
        _, velocity, _, pressure = primitive(flow)
        along_y = flux_along(flow, velocity, pressure, 1)
        along_z = flux_along(flow, velocity, pressure, 2)
        for c in range(5):
            q, y, z = flow[c], along_y[c], along_z[c]
            far = jnp.where(lane < 2, 0.0, -DAMP * q)
            plus = roll_lanes(jnp.where(lane == 0, 0.0, -SPEED * y + 4.0 * DAMP * q), -1)
            minus_1 = roll_lanes(jnp.where(lane == 127, 0.0, SPEED * y + 4.0 * DAMP * q), 1)
            plus = plus + roll_lanes(far, -2)
            minus_1 = minus_1 + roll_lanes(jnp.where(lane >= 126, 0.0, -DAMP * q), 2)
            z_plus = jnp.where(depth == 3, roll_rows(z, 3), roll_rows(z, -1))
            z_minus = jnp.where(depth == 0, roll_rows(z, -3), roll_rows(z, 1))
            partial = (plus + minus_1) - SPEED * (z_plus - z_minus) - 6.0 * DAMP * q
            both[c][2 * xh] = jnp.where(row < 4, q, roll_rows(partial, 4))
            both[c][2 * xh + 1] = jnp.where(row < 4, roll_rows(q, 4), partial)
    for c in range(5):
        tiles = swap_bit(swap_bit(swap_bit(both[c], 4, 64), 2, 32), 1, 16)
        for g in range(8):
            out_ref[pl.ds(g * 10 + c, 4, stride=80), :] = tiles[g][0:4]
            out_ref[pl.ds(g * 10 + 5 + c, 4, stride=80), :] = tiles[g][4:8]


def border_kernel(packed_ref, left_ref, right_ref, out_ref):
    place = lane_index() & 15
    top = row_index() < 4
    distance = jnp.where(top, 15 - place, place)
    nearest = distance == 0
    next_two = distance < 2
    sign = jnp.where(top, SPEED, -SPEED)
    flow = []
    for c in range(5):
        flow.append(jnp.where(top, left_ref[8 * c : 8 * c + 8, :], right_ref[8 * c : 8 * c + 8, :]))
    _, velocity, _, pressure = primitive(flow)
    along_y = flux_along(flow, velocity, pressure, 1)
    for c in range(5):
        first = jnp.where(nearest, sign * along_y[c] + 4.0 * DAMP * flow[c], 0.0)
        second = jnp.where(next_two, -DAMP * flow[c], 0.0)
        total = jnp.where(
            top,
            roll_lanes(first, -15) + roll_lanes(second, -14),
            roll_lanes(first, 15) + roll_lanes(second, 14),
        )
        for j, g in ((0, 0), (1, 7)):
            rows = pl.ds(g * 10 + 5 + c, 4, stride=80)
            out_ref[rows, :] = packed_ref[rows, :] + total[4 * j : 4 * j + 4]


def swapped_halves(value):
    return roll_rows(value, 4)


def in_top(top, bottom):
    return jnp.where(row_index() < 4, top, bottom)


def half_before(value, periodic=False):
    turned = roll_lanes(value, 16)
    carried = roll_rows(turned, 5)
    if periodic:
        carried = jnp.where(row_index() == 0, roll_rows(turned, 1), carried)
    earlier = jnp.where(lane_index() < 16, carried, roll_rows(turned, 4))
    return in_top(earlier, roll_rows(value, 4))


def half_after(value, periodic=False):
    turned = roll_lanes(value, -16)
    carried = roll_rows(turned, 3)
    if periodic:
        carried = jnp.where(row_index() == 7, roll_rows(turned, 7), carried)
    later = jnp.where(lane_index() >= 112, carried, roll_rows(turned, 4))
    return in_top(roll_rows(value, 4), later)


def blocks_before(value, stride):
    if stride >= 8:
        return roll_rows(value, stride // 8)
    turned = roll_lanes(value, 16 * stride)
    return jnp.where(lane_index() < 16 * stride, roll_rows(turned, 1), turned)


def blocks_after(value, stride):
    if stride >= 8:
        return roll_rows(value, -(stride // 8))
    turned = roll_lanes(value, -16 * stride)
    return jnp.where(lane_index() >= 128 - 16 * stride, roll_rows(turned, -1), turned)


def jacobian_entries(flow):
    inverse, velocity, squared, pressure = primitive(flow)
    u, v, w = velocity
    f = 0.2 * squared
    h = (flow[4] + pressure) * inverse
    return [
        [None, 1.0, None, None, None],
        [f - u * u, 1.6 * u, -0.4 * v, -0.4 * w, 0.4],
        [-u * v, v, u, None, None],
        [-u * w, w, None, u, None],
        [u * (f - h), h - 0.4 * u * u, -0.4 * u * v, -0.4 * u * w, 1.4 * u],
    ], velocity, pressure


def scaled_plus(table, factor, shift):
    result = []
    for i in range(5):
        entries = []
        for j in range(5):
            entry = table[i][j]
            entry = None if entry is None else factor * entry
            if i == j:
                entry = shift if entry is None else entry + shift
            entries.append(entry)
        result.append(entries)
    return result


def kept_where(mask, table):
    return [[None if e is None else jnp.where(mask, e, 0.0) for e in row] for row in table]


def multiply(former, latter):
    columns = len(latter[0])
    result = []
    for i in range(5):
        entries = []
        for j in range(columns):
            total = None
            for k in range(5):
                if former[i][k] is None or latter[k][j] is None:
                    continue
                term = former[i][k] * latter[k][j]
                total = term if total is None else total + term
            entries.append(total)
        result.append(entries)
    return result


def add_tables(first, second):
    return [
        [b if a is None else (a if b is None else a + b) for a, b in zip(x, y)]
        for x, y in zip(first, second)
    ]


def identity_minus(table):
    return [[(1.0 - table[i][j]) if i == j else -table[i][j] for j in range(5)] for i in range(5)]


def dense(table):
    return [[e if hasattr(e, "shape") else jnp.full((8, 128), e, jnp.float32) for e in row] for row in table]


def solve(matrix, source):
    rows = [list(matrix[i]) + list(source[i]) for i in range(5)]
    width = len(rows[0])
    for k in range(5):
        if k < 4:
            largest = jnp.abs(rows[k][k])
            for j in range(k + 1, 5):
                candidate = jnp.abs(rows[j][k])
                better = candidate > largest
                largest = jnp.maximum(candidate, largest)
                for m in range(k, width):
                    upper, lower = rows[k][m], rows[j][m]
                    rows[k][m] = jnp.where(better, lower, upper)
                    rows[j][m] = jnp.where(better, upper, lower)
        inverse = 1.0 / rows[k][k]
        for m in range(k + 1, width):
            rows[k][m] = rows[k][m] * inverse
        for i in range(k + 1, 5):
            factor = rows[i][k]
            for m in range(k + 1, width):
                rows[i][m] = rows[i][m] - factor * rows[k][m]
    for k in range(4, 0, -1):
        for i in range(k):
            factor = rows[i][k]
            for m in range(5, width):
                rows[i][m] = rows[i][m] - factor * rows[k][m]
    return [rows[i][5:] for i in range(5)]


def side_by_side(*tables):
    return [sum((list(t[i]) for t in tables), []) for i in range(5)]


def columns_of(table, begin, end):
    return [row[begin:end] for row in table]


def mapped(function, table):
    return [[function(e) for e in row] for row in table]


def both_halves(table):
    return mapped(lambda e: e + swapped_halves(e), table)


def minus(first, second):
    return [[a - b for a, b in zip(x, y)] for x, y in zip(first, second)]


def line_kernel(received_ref, out_ref):
    lane = lane_index()
    row = row_index()
    first_half = (row == 0) & (lane < 16)
    last_half = (row == 7) & (lane >= 112)
    straight = (row >= 4) == (lane >= 64)

    def exchanged(tile):
        return jnp.where(straight, tile, roll_lanes(swapped_halves(tile), 64))

    def load(position):
        tiles = []
        for u in range(4):
            halves = [
                received_ref[pl.ds((u + 4 * j) * 10 + position, 4, stride=80), :] for j in range(2)
            ]
            tiles.append(exchanged(jnp.concatenate(halves, axis=0)))
        return swap_bit(swap_bit(tiles, 2, 32), 1, 16)

    flow = [load(c) for c in range(5)]
    partial = [load(5 + c) for c in range(5)]
    cells = {t: [flow[c][t] for c in range(5)] for t in range(4)}
    cells[-2] = [half_before(e, True) for e in cells[2]]
    cells[-1] = [half_before(e, True) for e in cells[3]]
    cells[4] = [half_after(e, True) for e in cells[0]]
    cells[5] = [half_after(e, True) for e in cells[1]]
    from_before, from_after, along_x = {}, {}, {}
    for t in range(-2, 5):
        table, velocity, pressure = jacobian_entries(cells[t])
        from_before[t] = scaled_plus(table, SCALE, SHARE)
        from_after[t] = scaled_plus(table, -SCALE, SHARE)
        along_x[t] = flux_along(cells[t], velocity, pressure, 0)
    from_before[-1] = kept_where(jnp.logical_not(first_half), from_before[-1])
    from_after[4] = kept_where(jnp.logical_not(last_half), from_after[4])
    right = {}
    for t in range(4):
        right[t] = []
        for c in range(5):
            fourth = (
                (cells[t + 2][c] + cells[t - 2][c])
                - 4.0 * (cells[t + 1][c] + cells[t - 1][c])
                + 6.0 * cells[t][c]
            )
            total = partial[c][t] - SPEED * (along_x[t + 1][c] - along_x[t - 1][c]) - DAMP * fourth
            right[t].append([total * SHARE])
    right[-1] = mapped(half_before, right[3])

    def eliminated(t):
        matrix = identity_minus(
            add_tables(
                multiply(from_after[t + 1], from_before[t]),
                multiply(from_before[t - 1], from_after[t]),
            )
        )
        before = dense(multiply(from_before[t - 1], from_before[t - 2]))
        after = dense(multiply(from_after[t + 1], from_after[t + 2]))
        value = add_tables(
            right[t],
            add_tables(
                multiply(from_after[t + 1], right[t + 1]), multiply(from_before[t - 1], right[t - 1])
            ),
        )
        return matrix, before, after, value

    matrix, before, after, value = eliminated(2)
    solved = solve(matrix, side_by_side(before, after, value))
    fine_before, fine_after, fine_value = (
        columns_of(solved, 0, 5), columns_of(solved, 5, 10), columns_of(solved, 10, 11)
    )
    matrix, before, after, value = eliminated(0)
    matrix = minus(
        matrix,
        add_tables(
            multiply(after, fine_before), multiply(before, mapped(half_before, fine_after))
        ),
    )
    value = add_tables(
        value,
        add_tables(multiply(after, fine_value), multiply(before, mapped(half_before, fine_value))),
    )
    before = multiply(before, mapped(half_before, fine_before))
    after = multiply(after, fine_after)

    def pick(table, function):
        return mapped(lambda e: function(e, swapped_halves(e)), table)

    packed = [[in_top(a, swapped_halves(b)) for a, b in zip(x, y)] for x, y in zip(before, after)]
    second = [[in_top(swapped_halves(a), b) for a, b in zip(x, y)] for x, y in zip(before, after)]
    second_matrix = pick(matrix, lambda e, swapped: in_top(swapped, e))
    second_value = pick(value, lambda e, swapped: in_top(swapped, e))
    matrix = pick(matrix, in_top)
    value = pick(value, in_top)
    solved = solve(second_matrix, side_by_side(second, second_value))
    second, second_value = columns_of(solved, 0, 5), columns_of(solved, 5, 6)

    def top_before(table):
        return mapped(lambda e: in_top(blocks_before(e, 1), e), table)

    matrix = minus(matrix, both_halves(multiply(packed, mapped(half_before, second))))
    value = add_tables(value, both_halves(multiply(packed, top_before(second_value))))
    packed = multiply(packed, top_before(second))
    solved = solve(matrix, side_by_side(packed, value))
    packed, value = columns_of(solved, 0, 5), columns_of(solved, 5, 6)

    stride = 1
    while stride < 32:
        earlier = lambda table: mapped(lambda e: blocks_before(e, stride), table)
        later = lambda table: mapped(lambda e: blocks_after(e, stride), table)
        towards = lambda x, y: [[in_top(a, b) for a, b in zip(p, q)] for p, q in zip(x, y)]
        prior, following = earlier(packed), later(packed)
        crossed = mapped(swapped_halves, towards(following, prior))
        matrix = identity_minus(both_halves(multiply(packed, crossed)))
        beside = towards(earlier(value), later(value))
        value = add_tables(value, both_halves(multiply(packed, beside)))
        if stride < 16:
            packed = multiply(packed, towards(prior, following))
            solved = solve(matrix, side_by_side(packed, value))
            packed, value = columns_of(solved, 0, 5), columns_of(solved, 5, 6)
        else:
            value = solve(matrix, value)
        stride *= 2

    last_block = ((row & 3) == 3) & (lane >= 112)
    ahead = mapped(lambda e: jnp.where(last_block, 0.0, blocks_after(e, 1)), value)
    around = [[in_top(a[0], b[0])] for a, b in zip(value, ahead)]
    middle = add_tables(second_value, both_halves(multiply(second, around)))
    result = {
        0: [[in_top(a[0], b[0])] for a, b in zip(value, middle)],
        4: [[in_top(a[0], b[0])] for a, b in zip(middle, ahead)],
    }
    result[2] = add_tables(
        fine_value, add_tables(multiply(fine_before, result[0]), multiply(fine_after, result[4]))
    )
    for t in (1, 3):
        result[t] = add_tables(
            right[t],
            add_tables(
                multiply(from_before[t - 1], result[t - 1]), multiply(from_after[t + 1], result[t + 1])
            ),
        )
    for c in range(5):
        tiles = swap_bit(swap_bit([result[t][c][0] for t in range(4)], 2, 32), 1, 16)
        for u in range(4):
            tile = exchanged(tiles[u])
            for j in range(2):
                out_ref[pl.ds((u + 4 * j) * 5 + c, 4, stride=40), :] = tile[4 * j : 4 * j + 4]


def unpack_kernel(returned_ref, out_ref):
    for c in range(5):
        tiles = [returned_ref[pl.ds(g * 5 + c, 4, stride=40), :] for g in range(8)]
        tiles = swap_bit(tiles, 4, 64)
        tiles = swap_bit(tiles, 2, 32)
        tiles = swap_bit(tiles, 1, 16)
        for x in range(8):
            out_ref[c * 32 + x * 4 : c * 32 + x * 4 + 4, :] = tiles[x]


def call(kernel, rows, *operands, **options):
    whole = pl.BlockSpec(memory_space=pltpu.VMEM)
    return pl.pallas_call(
        kernel,
        out_shape=jax.ShapeDtypeStruct((rows, 128), jnp.float32),
        in_specs=[whole] * len(operands),
        out_specs=whole,
        compiler_params=pltpu.CompilerParams(vmem_limit_bytes=32 * 1024 * 1024),
        **options,
    )(*operands)


def per_device(flow_state):
    flow = flow_state.reshape(160, 128)
    count = lax.axis_size("gy")
    edge = call(edge_kernel, 40, flow)
    left = lax.ppermute(edge, "gy", [(i, (i + 1) % count) for i in range(count)])
    right = lax.ppermute(edge, "gy", [((i + 1) % count, i) for i in range(count)])
    cost = pl.CostEstimate(flops=4000000, bytes_accessed=250000, transcendentals=0)
    packed = call(pack_kernel, 320, flow, cost_estimate=cost)
    packed = call(border_kernel, 320, packed, left, right, input_output_aliases={0: 0})
    received = lax.all_to_all(
        packed.reshape(32, 1, 1280), "gx", split_axis=0, concat_axis=0, tiled=True
    ).reshape(320, 128)
    solved = call(line_kernel, 160, received)
    returned = lax.all_to_all(
        solved.reshape(32, 1, 640), "gx", split_axis=0, concat_axis=0, tiled=True
    ).reshape(160, 128)
    return call(unpack_kernel, 160, returned).reshape(flow_state.shape)


def solution(mesh):
    placed = (P(None, "gx", None, "gy"),)
    return jax.shard_map(
        per_device, mesh=mesh, in_specs=placed, out_specs=P(None, "gx", None, "gy"), check_vma=False
    )
```

```python
import jax
import jax.numpy as jnp
from jax import lax
from jax.experimental import pallas as pl
from jax.experimental.pallas import tpu as pltpu
from jax.sharding import PartitionSpec as P

SPEED = 20.0
DAMP = 0.05
SCALE = SPEED / 3.0
SHARE = 1.0 / 3.0


def roll_lanes(value, amount):
    return value if amount % 128 == 0 else pltpu.roll(value, amount % 128, 1)


def roll_rows(value, amount):
    return value if amount % 8 == 0 else pltpu.roll(value, amount % 8, 0)


def lane_index():
    return lax.broadcasted_iota(jnp.int32, (8, 128), 1)


def row_index():
    return lax.broadcasted_iota(jnp.int32, (8, 128), 0)


def swap_bit(tiles, bit, width):
    shape = tiles[0].shape
    low = (lax.broadcasted_iota(jnp.int32, shape, 1) & width) == 0
    swapped = list(tiles)
    for i in range(len(tiles)):
        if not i & bit:
            first, second = tiles[i], tiles[i | bit]
            swapped[i] = jnp.where(low, first, roll_lanes(second, width))
            swapped[i | bit] = jnp.where(low, roll_lanes(first, -width), second)
    return swapped


def primitive(flow):
    inverse = 1.0 / flow[0]
    velocity = [flow[1] * inverse, flow[2] * inverse, flow[3] * inverse]
    squared = velocity[0] * velocity[0] + velocity[1] * velocity[1] + velocity[2] * velocity[2]
    pressure = 0.4 * (flow[4] - 0.5 * flow[0] * squared)
    return inverse, velocity, squared, pressure


def flux_along(flow, velocity, pressure, direction):
    moving = velocity[direction]
    pieces = [
        flow[1 + direction],
        flow[1] * moving,
        flow[2] * moving,
        flow[3] * moving,
        (flow[4] + pressure) * moving,
    ]
    pieces[1 + direction] = pieces[1 + direction] + pressure
    return pieces


def edge_kernel(flow_ref, edge_ref):
    lane = lane_index()
    top = row_index() < 4
    for c in range(5):
        packed = None
        for xh in range(4):
            v = c * 4 + xh
            tile = flow_ref[8 * v : 8 * v + 8, :]
            turned = roll_lanes(tile, 16)
            for xl in range(2):
                if xl == 0:
                    chosen = jnp.where(top, turned, roll_rows(tile, 4))
                else:
                    chosen = jnp.where(top, roll_rows(turned, 4), tile)
                x = 2 * xh + xl
                chosen = roll_lanes(chosen, 16 * x)
                packed = chosen if packed is None else jnp.where(lane >= 16 * x, chosen, packed)
        edge_ref[8 * c : 8 * c + 8, :] = packed


def pack_kernel(flow_ref, out_ref):
    lane = lane_index()
    row = row_index()
    depth = row & 3
    both = [[None] * 8 for _ in range(5)]
    for xh in range(4):
        flow = []
        for c in range(5):
            v = c * 4 + xh
            flow.append(flow_ref[8 * v : 8 * v + 8, :])
        _, velocity, _, pressure = primitive(flow)
        along_y = flux_along(flow, velocity, pressure, 1)
        along_z = flux_along(flow, velocity, pressure, 2)
        for c in range(5):
            q, y, z = flow[c], along_y[c], along_z[c]
            far = jnp.where(lane < 2, 0.0, -DAMP * q)
            plus = roll_lanes(jnp.where(lane == 0, 0.0, -SPEED * y + 4.0 * DAMP * q), -1)
            minus_1 = roll_lanes(jnp.where(lane == 127, 0.0, SPEED * y + 4.0 * DAMP * q), 1)
            plus = plus + roll_lanes(far, -2)
            minus_1 = minus_1 + roll_lanes(jnp.where(lane >= 126, 0.0, -DAMP * q), 2)
            z_plus = jnp.where(depth == 3, roll_rows(z, 3), roll_rows(z, -1))
            z_minus = jnp.where(depth == 0, roll_rows(z, -3), roll_rows(z, 1))
            partial = (plus + minus_1) - SPEED * (z_plus - z_minus) - 6.0 * DAMP * q
            both[c][2 * xh] = jnp.where(row < 4, q, roll_rows(partial, 4))
            both[c][2 * xh + 1] = jnp.where(row < 4, roll_rows(q, 4), partial)
    for c in range(5):
        tiles = swap_bit(swap_bit(swap_bit(both[c], 4, 64), 2, 32), 1, 16)
        for g in range(8):
            out_ref[pl.ds(g * 10 + c, 4, stride=80), :] = tiles[g][0:4]
            out_ref[pl.ds(g * 10 + 5 + c, 4, stride=80), :] = tiles[g][4:8]


def border_kernel(packed_ref, odd_ref, even_ref, out_ref):
    is_top = (row_index() < 4).astype(jnp.int32)
    by_odd = is_top == lax.rem(lax.axis_index("gy"), 2)
    place = lane_index() & 15
    top = row_index() < 4
    distance = jnp.where(top, 15 - place, place)
    nearest = distance == 0
    next_two = distance < 2
    sign = jnp.where(top, SPEED, -SPEED)
    flow = []
    for c in range(5):
        flow.append(jnp.where(by_odd, odd_ref[8 * c : 8 * c + 8, :], even_ref[8 * c : 8 * c + 8, :]))
    _, velocity, _, pressure = primitive(flow)
    along_y = flux_along(flow, velocity, pressure, 1)
    for c in range(5):
        first = jnp.where(nearest, sign * along_y[c] + 4.0 * DAMP * flow[c], 0.0)
        second = jnp.where(next_two, -DAMP * flow[c], 0.0)
        total = jnp.where(
            top,
            roll_lanes(first, -15) + roll_lanes(second, -14),
            roll_lanes(first, 15) + roll_lanes(second, 14),
        )
        for j, g in ((0, 0), (1, 7)):
            rows = pl.ds(g * 10 + 5 + c, 4, stride=80)
            out_ref[rows, :] = packed_ref[rows, :] + total[4 * j : 4 * j + 4]


def swapped_halves(value):
    return roll_rows(value, 4)


def in_top(top, bottom):
    return jnp.where(row_index() < 4, top, bottom)


def half_before(value, periodic=False):
    turned = roll_lanes(value, 16)
    carried = roll_rows(turned, 5)
    if periodic:
        carried = jnp.where(row_index() == 0, roll_rows(turned, 1), carried)
    earlier = jnp.where(lane_index() < 16, carried, roll_rows(turned, 4))
    return in_top(earlier, roll_rows(value, 4))


def half_after(value, periodic=False):
    turned = roll_lanes(value, -16)
    carried = roll_rows(turned, 3)
    if periodic:
        carried = jnp.where(row_index() == 7, roll_rows(turned, 7), carried)
    later = jnp.where(lane_index() >= 112, carried, roll_rows(turned, 4))
    return in_top(roll_rows(value, 4), later)


def blocks_before(value, stride):
    if stride >= 8:
        return roll_rows(value, stride // 8)
    turned = roll_lanes(value, 16 * stride)
    return jnp.where(lane_index() < 16 * stride, roll_rows(turned, 1), turned)


def blocks_after(value, stride):
    if stride >= 8:
        return roll_rows(value, -(stride // 8))
    turned = roll_lanes(value, -16 * stride)
    return jnp.where(lane_index() >= 128 - 16 * stride, roll_rows(turned, -1), turned)


def jacobian_entries(flow):
    inverse, velocity, squared, pressure = primitive(flow)
    u, v, w = velocity
    f = 0.2 * squared
    h = (flow[4] + pressure) * inverse
    return [
        [None, 1.0, None, None, None],
        [f - u * u, 1.6 * u, -0.4 * v, -0.4 * w, 0.4],
        [-u * v, v, u, None, None],
        [-u * w, w, None, u, None],
        [u * (f - h), h - 0.4 * u * u, -0.4 * u * v, -0.4 * u * w, 1.4 * u],
    ], velocity, pressure


def scaled_plus(table, factor, shift):
    result = []
    for i in range(5):
        entries = []
        for j in range(5):
            entry = table[i][j]
            entry = None if entry is None else factor * entry
            if i == j:
                entry = shift if entry is None else entry + shift
            entries.append(entry)
        result.append(entries)
    return result


def kept_where(mask, table):
    return [[None if e is None else jnp.where(mask, e, 0.0) for e in row] for row in table]


def multiply(former, latter):
    columns = len(latter[0])
    result = []
    for i in range(5):
        entries = []
        for j in range(columns):
            total = None
            for k in range(5):
                if former[i][k] is None or latter[k][j] is None:
                    continue
                term = former[i][k] * latter[k][j]
                total = term if total is None else total + term
            entries.append(total)
        result.append(entries)
    return result


def add_tables(first, second):
    return [
        [b if a is None else (a if b is None else a + b) for a, b in zip(x, y)]
        for x, y in zip(first, second)
    ]


def identity_minus(table):
    return [[(1.0 - table[i][j]) if i == j else -table[i][j] for j in range(5)] for i in range(5)]


def dense(table):
    return [[e if hasattr(e, "shape") else jnp.full((8, 128), e, jnp.float32) for e in row] for row in table]


def solve(matrix, source):
    rows = [list(matrix[i]) + list(source[i]) for i in range(5)]
    width = len(rows[0])
    for k in range(5):
        if k < 4:
            largest = jnp.abs(rows[k][k])
            for j in range(k + 1, 5):
                candidate = jnp.abs(rows[j][k])
                better = candidate > largest
                largest = jnp.maximum(candidate, largest)
                for m in range(k, width):
                    upper, lower = rows[k][m], rows[j][m]
                    rows[k][m] = jnp.where(better, lower, upper)
                    rows[j][m] = jnp.where(better, upper, lower)
        inverse = 1.0 / rows[k][k]
        for m in range(k + 1, width):
            rows[k][m] = rows[k][m] * inverse
        for i in range(k + 1, 5):
            factor = rows[i][k]
            for m in range(k + 1, width):
                rows[i][m] = rows[i][m] - factor * rows[k][m]
    for k in range(4, 0, -1):
        for i in range(k):
            factor = rows[i][k]
            for m in range(5, width):
                rows[i][m] = rows[i][m] - factor * rows[k][m]
    return [rows[i][5:] for i in range(5)]


def side_by_side(*tables):
    return [sum((list(t[i]) for t in tables), []) for i in range(5)]


def columns_of(table, begin, end):
    return [row[begin:end] for row in table]


def mapped(function, table):
    return [[function(e) for e in row] for row in table]


def both_halves(table):
    return mapped(lambda e: e + swapped_halves(e), table)


def minus(first, second):
    return [[a - b for a, b in zip(x, y)] for x, y in zip(first, second)]


def line_kernel(received_ref, out_ref):
    lane = lane_index()
    row = row_index()
    first_half = (row == 0) & (lane < 16)
    last_half = (row == 7) & (lane >= 112)
    straight = (row >= 4) == (lane >= 64)

    def exchanged(tile):
        return jnp.where(straight, tile, roll_lanes(swapped_halves(tile), 64))

    def load(position):
        tiles = []
        for u in range(4):
            halves = [
                received_ref[pl.ds((u + 4 * j) * 10 + position, 4, stride=80), :] for j in range(2)
            ]
            tiles.append(exchanged(jnp.concatenate(halves, axis=0)))
        return swap_bit(swap_bit(tiles, 2, 32), 1, 16)

    flow = [load(c) for c in range(5)]
    partial = [load(5 + c) for c in range(5)]
    cells = {t: [flow[c][t] for c in range(5)] for t in range(4)}
    cells[-2] = [half_before(e, True) for e in cells[2]]
    cells[-1] = [half_before(e, True) for e in cells[3]]
    cells[4] = [half_after(e, True) for e in cells[0]]
    cells[5] = [half_after(e, True) for e in cells[1]]
    from_before, from_after, along_x = {}, {}, {}
    for t in range(-2, 5):
        table, velocity, pressure = jacobian_entries(cells[t])
        from_before[t] = scaled_plus(table, SCALE, SHARE)
        from_after[t] = scaled_plus(table, -SCALE, SHARE)
        along_x[t] = flux_along(cells[t], velocity, pressure, 0)
    from_before[-1] = kept_where(jnp.logical_not(first_half), from_before[-1])
    from_after[4] = kept_where(jnp.logical_not(last_half), from_after[4])
    right = {}
    for t in range(4):
        right[t] = []
        for c in range(5):
            fourth = (
                (cells[t + 2][c] + cells[t - 2][c])
                - 4.0 * (cells[t + 1][c] + cells[t - 1][c])
                + 6.0 * cells[t][c]
            )
            total = partial[c][t] - SPEED * (along_x[t + 1][c] - along_x[t - 1][c]) - DAMP * fourth
            right[t].append([total * SHARE])
    right[-1] = mapped(half_before, right[3])

    def eliminated(t):
        matrix = identity_minus(
            add_tables(
                multiply(from_after[t + 1], from_before[t]),
                multiply(from_before[t - 1], from_after[t]),
            )
        )
        before = dense(multiply(from_before[t - 1], from_before[t - 2]))
        after = dense(multiply(from_after[t + 1], from_after[t + 2]))
        value = add_tables(
            right[t],
            add_tables(
                multiply(from_after[t + 1], right[t + 1]), multiply(from_before[t - 1], right[t - 1])
            ),
        )
        return matrix, before, after, value

    matrix, before, after, value = eliminated(2)
    solved = solve(matrix, side_by_side(before, after, value))
    fine_before, fine_after, fine_value = (
        columns_of(solved, 0, 5), columns_of(solved, 5, 10), columns_of(solved, 10, 11)
    )
    matrix, before, after, value = eliminated(0)
    matrix = minus(
        matrix,
        add_tables(
            multiply(after, fine_before), multiply(before, mapped(half_before, fine_after))
        ),
    )
    value = add_tables(
        value,
        add_tables(multiply(after, fine_value), multiply(before, mapped(half_before, fine_value))),
    )
    before = multiply(before, mapped(half_before, fine_before))
    after = multiply(after, fine_after)

    def pick(table, function):
        return mapped(lambda e: function(e, swapped_halves(e)), table)

    packed = [[in_top(a, swapped_halves(b)) for a, b in zip(x, y)] for x, y in zip(before, after)]
    second = [[in_top(swapped_halves(a), b) for a, b in zip(x, y)] for x, y in zip(before, after)]
    second_matrix = pick(matrix, lambda e, swapped: in_top(swapped, e))
    second_value = pick(value, lambda e, swapped: in_top(swapped, e))
    matrix = pick(matrix, in_top)
    value = pick(value, in_top)
    solved = solve(second_matrix, side_by_side(second, second_value))
    second, second_value = columns_of(solved, 0, 5), columns_of(solved, 5, 6)

    def top_before(table):
        return mapped(lambda e: in_top(blocks_before(e, 1), e), table)

    matrix = minus(matrix, both_halves(multiply(packed, mapped(half_before, second))))
    value = add_tables(value, both_halves(multiply(packed, top_before(second_value))))
    packed = multiply(packed, top_before(second))
    solved = solve(matrix, side_by_side(packed, value))
    packed, value = columns_of(solved, 0, 5), columns_of(solved, 5, 6)

    stride = 1
    while stride < 32:
        earlier = lambda table: mapped(lambda e: blocks_before(e, stride), table)
        later = lambda table: mapped(lambda e: blocks_after(e, stride), table)
        towards = lambda x, y: [[in_top(a, b) for a, b in zip(p, q)] for p, q in zip(x, y)]
        prior, following = earlier(packed), later(packed)
        crossed = mapped(swapped_halves, towards(following, prior))
        matrix = identity_minus(both_halves(multiply(packed, crossed)))
        beside = towards(earlier(value), later(value))
        value = add_tables(value, both_halves(multiply(packed, beside)))
        if stride < 16:
            packed = multiply(packed, towards(prior, following))
            solved = solve(matrix, side_by_side(packed, value))
            packed, value = columns_of(solved, 0, 5), columns_of(solved, 5, 6)
        else:
            value = solve(matrix, value)
        stride *= 2

    last_block = ((row & 3) == 3) & (lane >= 112)
    ahead = mapped(lambda e: jnp.where(last_block, 0.0, blocks_after(e, 1)), value)
    around = [[in_top(a[0], b[0])] for a, b in zip(value, ahead)]
    middle = add_tables(second_value, both_halves(multiply(second, around)))
    result = {
        0: [[in_top(a[0], b[0])] for a, b in zip(value, middle)],
        4: [[in_top(a[0], b[0])] for a, b in zip(middle, ahead)],
    }
    result[2] = add_tables(
        fine_value, add_tables(multiply(fine_before, result[0]), multiply(fine_after, result[4]))
    )
    for t in (1, 3):
        result[t] = add_tables(
            right[t],
            add_tables(
                multiply(from_before[t - 1], result[t - 1]), multiply(from_after[t + 1], result[t + 1])
            ),
        )
    for c in range(5):
        tiles = swap_bit(swap_bit([result[t][c][0] for t in range(4)], 2, 32), 1, 16)
        for u in range(4):
            tile = exchanged(tiles[u])
            for j in range(2):
                out_ref[pl.ds((u + 4 * j) * 5 + c, 4, stride=40), :] = tile[4 * j : 4 * j + 4]


def unpack_kernel(returned_ref, out_ref):
    for c in range(5):
        tiles = [returned_ref[pl.ds(g * 5 + c, 4, stride=40), :] for g in range(8)]
        tiles = swap_bit(tiles, 4, 64)
        tiles = swap_bit(tiles, 2, 32)
        tiles = swap_bit(tiles, 1, 16)
        for x in range(8):
            out_ref[c * 32 + x * 4 : c * 32 + x * 4 + 4, :] = tiles[x]


def call(kernel, rows, *operands, **options):
    whole = pl.BlockSpec(memory_space=pltpu.VMEM)
    return pl.pallas_call(
        kernel,
        out_shape=jax.ShapeDtypeStruct((rows, 128), jnp.float32),
        in_specs=[whole] * len(operands),
        out_specs=whole,
        compiler_params=pltpu.CompilerParams(vmem_limit_bytes=32 * 1024 * 1024),
        **options,
    )(*operands)


def per_device(flow_state):
    flow = flow_state.reshape(160, 128)
    count = lax.axis_size("gy")
    edge = call(edge_kernel, 40, flow)
    exchanges = []
    for start in (0, 1):
        pairs = [((start + i) % count, (start + i + 1) % count) for i in range(0, count, 2)]
        exchanges.append(lax.ppermute(edge, "gy", pairs + [(b, a) for a, b in pairs]))
    cost = pl.CostEstimate(flops=4000000, bytes_accessed=250000, transcendentals=0)
    packed = call(pack_kernel, 320, flow, cost_estimate=cost)
    packed = call(border_kernel, 320, packed, *exchanges, input_output_aliases={0: 0})
    received = lax.all_to_all(
        packed.reshape(32, 1, 1280), "gx", split_axis=0, concat_axis=0, tiled=True
    ).reshape(320, 128)
    solved = call(line_kernel, 160, received)
    returned = lax.all_to_all(
        solved.reshape(32, 1, 640), "gx", split_axis=0, concat_axis=0, tiled=True
    ).reshape(160, 128)
    return call(unpack_kernel, 160, returned).reshape(flow_state.shape)


def solution(mesh):
    placed = (P(None, "gx", None, "gy"),)
    return jax.shard_map(
        per_device, mesh=mesh, in_specs=placed, out_specs=P(None, "gx", None, "gy"), check_vma=False
    )
```

```python
import jax
import jax.numpy as jnp
from jax import lax
from jax.experimental import pallas as pl
from jax.experimental.pallas import tpu as pltpu
from jax.sharding import PartitionSpec as P

SPEED = 20.0
DAMP = 0.05
SCALE = SPEED / 3.0
SHARE = 1.0 / 3.0


def roll_lanes(value, amount):
    return value if amount % 128 == 0 else pltpu.roll(value, amount % 128, 1)


def roll_rows(value, amount):
    return value if amount % 8 == 0 else pltpu.roll(value, amount % 8, 0)


def lane_index():
    return lax.broadcasted_iota(jnp.int32, (8, 128), 1)


def row_index():
    return lax.broadcasted_iota(jnp.int32, (8, 128), 0)


def swap_bit(tiles, bit, width):
    shape = tiles[0].shape
    low = (lax.broadcasted_iota(jnp.int32, shape, 1) & width) == 0
    swapped = list(tiles)
    for i in range(len(tiles)):
        if not i & bit:
            first, second = tiles[i], tiles[i | bit]
            swapped[i] = jnp.where(low, first, roll_lanes(second, width))
            swapped[i | bit] = jnp.where(low, roll_lanes(first, -width), second)
    return swapped


def primitive(flow):
    inverse = 1.0 / flow[0]
    velocity = [flow[1] * inverse, flow[2] * inverse, flow[3] * inverse]
    squared = velocity[0] * velocity[0] + velocity[1] * velocity[1] + velocity[2] * velocity[2]
    pressure = 0.4 * (flow[4] - 0.5 * flow[0] * squared)
    return inverse, velocity, squared, pressure


def flux_along(flow, velocity, pressure, direction):
    moving = velocity[direction]
    pieces = [
        flow[1 + direction],
        flow[1] * moving,
        flow[2] * moving,
        flow[3] * moving,
        (flow[4] + pressure) * moving,
    ]
    pieces[1 + direction] = pieces[1 + direction] + pressure
    return pieces


def edge_kernel(*refs):
    flow_refs, (odd_ref, even_ref) = refs[:5], refs[5:]
    swapped_by = jnp.zeros((8, 128), jnp.int32) + lax.rem(lax.axis_index("gy"), 2) == 1
    lane = lane_index()
    top = row_index() < 4
    for c in range(5):
        packed = None
        for xh in range(4):
            tile = flow_refs[c][8 * xh : 8 * xh + 8, :]
            turned = roll_lanes(tile, 16)
            for xl in range(2):
                if xl == 0:
                    chosen = jnp.where(top, turned, roll_rows(tile, 4))
                else:
                    chosen = jnp.where(top, roll_rows(turned, 4), tile)
                x = 2 * xh + xl
                chosen = roll_lanes(chosen, 16 * x)
                packed = chosen if packed is None else jnp.where(lane >= 16 * x, chosen, packed)
        turned = jnp.where(swapped_by, roll_rows(packed, 4), packed)
        odd_ref[4 * c : 4 * c + 4, :] = turned[0:4]
        even_ref[4 * c : 4 * c + 4, :] = turned[4:8]


def pack_kernel(*refs):
    flow_refs, out_ref = refs[:5], refs[5]
    lane = lane_index()
    row = row_index()
    depth = row & 3
    both = [[None] * 8 for _ in range(5)]
    for xh in range(4):
        flow = []
        for c in range(5):
            flow.append(flow_refs[c][8 * xh : 8 * xh + 8, :])
        _, velocity, _, pressure = primitive(flow)
        along_y = flux_along(flow, velocity, pressure, 1)
        along_z = flux_along(flow, velocity, pressure, 2)
        for c in range(5):
            q, y, z = flow[c], along_y[c], along_z[c]
            far = jnp.where(lane < 2, 0.0, -DAMP * q)
            plus = roll_lanes(jnp.where(lane == 0, 0.0, -SPEED * y + 4.0 * DAMP * q), -1)
            minus_1 = roll_lanes(jnp.where(lane == 127, 0.0, SPEED * y + 4.0 * DAMP * q), 1)
            plus = plus + roll_lanes(far, -2)
            minus_1 = minus_1 + roll_lanes(jnp.where(lane >= 126, 0.0, -DAMP * q), 2)
            z_plus = jnp.where(depth == 3, roll_rows(z, 3), roll_rows(z, -1))
            z_minus = jnp.where(depth == 0, roll_rows(z, -3), roll_rows(z, 1))
            partial = (plus + minus_1) - SPEED * (z_plus - z_minus) - 6.0 * DAMP * q
            both[c][2 * xh] = jnp.where(row < 4, q, roll_rows(partial, 4))
            both[c][2 * xh + 1] = jnp.where(row < 4, roll_rows(q, 4), partial)
    for c in range(5):
        tiles = swap_bit(swap_bit(swap_bit(both[c], 4, 64), 2, 32), 1, 16)
        for g in range(8):
            out_ref[pl.ds(g * 10 + c, 4, stride=80), :] = tiles[g][0:4]
            out_ref[pl.ds(g * 10 + 5 + c, 4, stride=80), :] = tiles[g][4:8]


def border_kernel(packed_ref, odd_ref, even_ref, out_ref):
    by_odd = jnp.zeros((8, 128), jnp.int32) + lax.rem(lax.axis_index("gy"), 2) == 1
    place = lane_index() & 15
    top = row_index() < 4
    distance = jnp.where(top, 15 - place, place)
    nearest = distance == 0
    next_two = distance < 2
    sign = jnp.where(top, SPEED, -SPEED)
    flow = []
    for c in range(5):
        beyond = [ref[4 * c : 4 * c + 4, :] for ref in (even_ref, odd_ref)]
        beyond = jnp.concatenate(beyond, axis=0)
        flow.append(jnp.where(by_odd, roll_rows(beyond, 4), beyond))
    _, velocity, _, pressure = primitive(flow)
    along_y = flux_along(flow, velocity, pressure, 1)
    for c in range(5):
        first = jnp.where(nearest, sign * along_y[c] + 4.0 * DAMP * flow[c], 0.0)
        second = jnp.where(next_two, -DAMP * flow[c], 0.0)
        total = jnp.where(
            top,
            roll_lanes(first, -15) + roll_lanes(second, -14),
            roll_lanes(first, 15) + roll_lanes(second, 14),
        )
        for j, g in ((0, 0), (1, 7)):
            rows = pl.ds(g * 10 + 5 + c, 4, stride=80)
            out_ref[rows, :] = packed_ref[rows, :] + total[4 * j : 4 * j + 4]


def swapped_halves(value):
    return roll_rows(value, 4)


def in_top(top, bottom):
    return jnp.where(row_index() < 4, top, bottom)


def half_before(value, periodic=False):
    turned = roll_lanes(value, 16)
    carried = roll_rows(turned, 5)
    if periodic:
        carried = jnp.where(row_index() == 0, roll_rows(turned, 1), carried)
    earlier = jnp.where(lane_index() < 16, carried, roll_rows(turned, 4))
    return in_top(earlier, roll_rows(value, 4))


def half_after(value, periodic=False):
    turned = roll_lanes(value, -16)
    carried = roll_rows(turned, 3)
    if periodic:
        carried = jnp.where(row_index() == 7, roll_rows(turned, 7), carried)
    later = jnp.where(lane_index() >= 112, carried, roll_rows(turned, 4))
    return in_top(roll_rows(value, 4), later)


def blocks_before(value, stride):
    if stride >= 8:
        return roll_rows(value, stride // 8)
    turned = roll_lanes(value, 16 * stride)
    return jnp.where(lane_index() < 16 * stride, roll_rows(turned, 1), turned)


def blocks_after(value, stride):
    if stride >= 8:
        return roll_rows(value, -(stride // 8))
    turned = roll_lanes(value, -16 * stride)
    return jnp.where(lane_index() >= 128 - 16 * stride, roll_rows(turned, -1), turned)


def jacobian_entries(flow):
    inverse, velocity, squared, pressure = primitive(flow)
    u, v, w = velocity
    f = 0.2 * squared
    h = (flow[4] + pressure) * inverse
    return [
        [None, 1.0, None, None, None],
        [f - u * u, 1.6 * u, -0.4 * v, -0.4 * w, 0.4],
        [-u * v, v, u, None, None],
        [-u * w, w, None, u, None],
        [u * (f - h), h - 0.4 * u * u, -0.4 * u * v, -0.4 * u * w, 1.4 * u],
    ], velocity, pressure


def scaled_plus(table, factor, shift):
    result = []
    for i in range(5):
        entries = []
        for j in range(5):
            entry = table[i][j]
            entry = None if entry is None else factor * entry
            if i == j:
                entry = shift if entry is None else entry + shift
            entries.append(entry)
        result.append(entries)
    return result


def kept_where(mask, table):
    return [[None if e is None else jnp.where(mask, e, 0.0) for e in row] for row in table]


def multiply(former, latter):
    columns = len(latter[0])
    result = []
    for i in range(5):
        entries = []
        for j in range(columns):
            total = None
            for k in range(5):
                if former[i][k] is None or latter[k][j] is None:
                    continue
                term = former[i][k] * latter[k][j]
                total = term if total is None else total + term
            entries.append(total)
        result.append(entries)
    return result


def add_tables(first, second):
    return [
        [b if a is None else (a if b is None else a + b) for a, b in zip(x, y)]
        for x, y in zip(first, second)
    ]


def identity_minus(table):
    return [[(1.0 - table[i][j]) if i == j else -table[i][j] for j in range(5)] for i in range(5)]


def dense(table):
    return [[e if hasattr(e, "shape") else jnp.full((8, 128), e, jnp.float32) for e in row] for row in table]


def solve(matrix, source):
    rows = [list(matrix[i]) + list(source[i]) for i in range(5)]
    width = len(rows[0])
    for k in range(5):
        if k < 4:
            largest = jnp.abs(rows[k][k])
            for j in range(k + 1, 5):
                candidate = jnp.abs(rows[j][k])
                better = candidate > largest
                largest = jnp.maximum(candidate, largest)
                for m in range(k, width):
                    upper, lower = rows[k][m], rows[j][m]
                    rows[k][m] = jnp.where(better, lower, upper)
                    rows[j][m] = jnp.where(better, upper, lower)
        inverse = 1.0 / rows[k][k]
        for m in range(k + 1, width):
            rows[k][m] = rows[k][m] * inverse
        for i in range(k + 1, 5):
            factor = rows[i][k]
            for m in range(k + 1, width):
                rows[i][m] = rows[i][m] - factor * rows[k][m]
    for k in range(4, 0, -1):
        for i in range(k):
            factor = rows[i][k]
            for m in range(5, width):
                rows[i][m] = rows[i][m] - factor * rows[k][m]
    return [rows[i][5:] for i in range(5)]


def side_by_side(*tables):
    return [sum((list(t[i]) for t in tables), []) for i in range(5)]


def columns_of(table, begin, end):
    return [row[begin:end] for row in table]


def mapped(function, table):
    return [[function(e) for e in row] for row in table]


def both_halves(table):
    return mapped(lambda e: e + swapped_halves(e), table)


def minus(first, second):
    return [[a - b for a, b in zip(x, y)] for x, y in zip(first, second)]


def line_kernel(received_ref, out_ref):
    lane = lane_index()
    row = row_index()
    first_half = (row == 0) & (lane < 16)
    last_half = (row == 7) & (lane >= 112)
    straight = (row >= 4) == (lane >= 64)

    def exchanged(tile):
        return jnp.where(straight, tile, roll_lanes(swapped_halves(tile), 64))

    def load(position):
        tiles = []
        for u in range(4):
            halves = [
                received_ref[pl.ds((u + 4 * j) * 10 + position, 4, stride=80), :] for j in range(2)
            ]
            tiles.append(exchanged(jnp.concatenate(halves, axis=0)))
        return swap_bit(swap_bit(tiles, 2, 32), 1, 16)

    flow = [load(c) for c in range(5)]
    partial = [load(5 + c) for c in range(5)]
    cells = {t: [flow[c][t] for c in range(5)] for t in range(4)}
    cells[-2] = [half_before(e, True) for e in cells[2]]
    cells[-1] = [half_before(e, True) for e in cells[3]]
    cells[4] = [half_after(e, True) for e in cells[0]]
    cells[5] = [half_after(e, True) for e in cells[1]]
    from_before, from_after, along_x = {}, {}, {}
    for t in range(-2, 5):
        table, velocity, pressure = jacobian_entries(cells[t])
        from_before[t] = scaled_plus(table, SCALE, SHARE)
        from_after[t] = scaled_plus(table, -SCALE, SHARE)
        along_x[t] = flux_along(cells[t], velocity, pressure, 0)
    from_before[-1] = kept_where(jnp.logical_not(first_half), from_before[-1])
    from_after[4] = kept_where(jnp.logical_not(last_half), from_after[4])
    right = {}
    for t in range(4):
        right[t] = []
        for c in range(5):
            fourth = (
                (cells[t + 2][c] + cells[t - 2][c])
                - 4.0 * (cells[t + 1][c] + cells[t - 1][c])
                + 6.0 * cells[t][c]
            )
            total = partial[c][t] - SPEED * (along_x[t + 1][c] - along_x[t - 1][c]) - DAMP * fourth
            right[t].append([total * SHARE])
    right[-1] = mapped(half_before, right[3])

    def eliminated(t):
        matrix = identity_minus(
            add_tables(
                multiply(from_after[t + 1], from_before[t]),
                multiply(from_before[t - 1], from_after[t]),
            )
        )
        before = dense(multiply(from_before[t - 1], from_before[t - 2]))
        after = dense(multiply(from_after[t + 1], from_after[t + 2]))
        value = add_tables(
            right[t],
            add_tables(
                multiply(from_after[t + 1], right[t + 1]), multiply(from_before[t - 1], right[t - 1])
            ),
        )
        return matrix, before, after, value

    matrix, before, after, value = eliminated(2)
    solved = solve(matrix, side_by_side(before, after, value))
    fine_before, fine_after, fine_value = (
        columns_of(solved, 0, 5), columns_of(solved, 5, 10), columns_of(solved, 10, 11)
    )
    matrix, before, after, value = eliminated(0)
    matrix = minus(
        matrix,
        add_tables(
            multiply(after, fine_before), multiply(before, mapped(half_before, fine_after))
        ),
    )
    value = add_tables(
        value,
        add_tables(multiply(after, fine_value), multiply(before, mapped(half_before, fine_value))),
    )
    before = multiply(before, mapped(half_before, fine_before))
    after = multiply(after, fine_after)

    def pick(table, function):
        return mapped(lambda e: function(e, swapped_halves(e)), table)

    packed = [[in_top(a, swapped_halves(b)) for a, b in zip(x, y)] for x, y in zip(before, after)]
    second = [[in_top(swapped_halves(a), b) for a, b in zip(x, y)] for x, y in zip(before, after)]
    second_matrix = pick(matrix, lambda e, swapped: in_top(swapped, e))
    second_value = pick(value, lambda e, swapped: in_top(swapped, e))
    matrix = pick(matrix, in_top)
    value = pick(value, in_top)
    solved = solve(second_matrix, side_by_side(second, second_value))
    second, second_value = columns_of(solved, 0, 5), columns_of(solved, 5, 6)

    def top_before(table):
        return mapped(lambda e: in_top(blocks_before(e, 1), e), table)

    matrix = minus(matrix, both_halves(multiply(packed, mapped(half_before, second))))
    value = add_tables(value, both_halves(multiply(packed, top_before(second_value))))
    packed = multiply(packed, top_before(second))
    solved = solve(matrix, side_by_side(packed, value))
    packed, value = columns_of(solved, 0, 5), columns_of(solved, 5, 6)

    stride = 1
    while stride < 32:
        earlier = lambda table: mapped(lambda e: blocks_before(e, stride), table)
        later = lambda table: mapped(lambda e: blocks_after(e, stride), table)
        towards = lambda x, y: [[in_top(a, b) for a, b in zip(p, q)] for p, q in zip(x, y)]
        prior, following = earlier(packed), later(packed)
        crossed = mapped(swapped_halves, towards(following, prior))
        matrix = identity_minus(both_halves(multiply(packed, crossed)))
        beside = towards(earlier(value), later(value))
        value = add_tables(value, both_halves(multiply(packed, beside)))
        if stride < 16:
            packed = multiply(packed, towards(prior, following))
            solved = solve(matrix, side_by_side(packed, value))
            packed, value = columns_of(solved, 0, 5), columns_of(solved, 5, 6)
        else:
            value = solve(matrix, value)
        stride *= 2

    last_block = ((row & 3) == 3) & (lane >= 112)
    ahead = mapped(lambda e: jnp.where(last_block, 0.0, blocks_after(e, 1)), value)
    around = [[in_top(a[0], b[0])] for a, b in zip(value, ahead)]
    middle = add_tables(second_value, both_halves(multiply(second, around)))
    result = {
        0: [[in_top(a[0], b[0])] for a, b in zip(value, middle)],
        4: [[in_top(a[0], b[0])] for a, b in zip(middle, ahead)],
    }
    result[2] = add_tables(
        fine_value, add_tables(multiply(fine_before, result[0]), multiply(fine_after, result[4]))
    )
    for t in (1, 3):
        result[t] = add_tables(
            right[t],
            add_tables(
                multiply(from_before[t - 1], result[t - 1]), multiply(from_after[t + 1], result[t + 1])
            ),
        )
    for c in range(5):
        tiles = swap_bit(swap_bit([result[t][c][0] for t in range(4)], 2, 32), 1, 16)
        for u in range(4):
            tile = exchanged(tiles[u])
            for j in range(2):
                out_ref[pl.ds((u + 4 * j) * 5 + c, 4, stride=40), :] = tile[4 * j : 4 * j + 4]


def unpack_kernel(returned_ref, out_ref):
    for c in range(5):
        tiles = [returned_ref[pl.ds(g * 5 + c, 4, stride=40), :] for g in range(8)]
        tiles = swap_bit(tiles, 4, 64)
        tiles = swap_bit(tiles, 2, 32)
        tiles = swap_bit(tiles, 1, 16)
        for x in range(8):
            out_ref[c * 32 + x * 4 : c * 32 + x * 4 + 4, :] = tiles[x]


def call(kernel, rows, *operands, **options):
    whole = pl.BlockSpec(memory_space=pltpu.VMEM)
    return pl.pallas_call(
        kernel,
        out_shape=jax.ShapeDtypeStruct((rows, 128), jnp.float32),
        in_specs=[whole] * len(operands),
        out_specs=whole,
        compiler_params=pltpu.CompilerParams(vmem_limit_bytes=32 * 1024 * 1024),
        **options,
    )(*operands)


def per_device(flow_state):
    flow = [flow_state[c].reshape(32, 128) for c in range(5)]
    count = lax.axis_size("gy")
    vmem = pl.BlockSpec(memory_space=pltpu.VMEM)
    edges = pl.pallas_call(
        edge_kernel,
        out_shape=[jax.ShapeDtypeStruct((20, 128), jnp.float32)] * 2,
        in_specs=[vmem] * 5,
        out_specs=[vmem] * 2,
        compiler_params=pltpu.CompilerParams(vmem_limit_bytes=32 * 1024 * 1024),
    )(*flow)
    exchanges = [None, None]
    for start in (1, 0):
        pairs = [((start + i) % count, (start + i + 1) % count) for i in range(0, count, 2)]
        exchanges[start] = lax.ppermute(edges[start], "gy", pairs + [(b, a) for a, b in pairs])
    cost = pl.CostEstimate(flops=4000000, bytes_accessed=250000, transcendentals=0)
    packed = call(pack_kernel, 320, *flow, cost_estimate=cost)
    packed = call(border_kernel, 320, packed, *exchanges, input_output_aliases={0: 0})
    received = lax.all_to_all(
        packed.reshape(32, 1, 1280), "gx", split_axis=0, concat_axis=0, tiled=True
    ).reshape(320, 128)
    solved = call(line_kernel, 160, received)
    returned = lax.all_to_all(
        solved.reshape(32, 1, 640), "gx", split_axis=0, concat_axis=0, tiled=True
    ).reshape(160, 128)
    return call(unpack_kernel, 160, returned).reshape(flow_state.shape)


def solution(mesh):
    placed = (P(None, "gx", None, "gy"),)
    return jax.shard_map(
        per_device, mesh=mesh, in_specs=placed, out_specs=P(None, "gx", None, "gy"), check_vma=False
    )
```

```python
import jax
import jax.numpy as jnp
from jax import lax
from jax.experimental import pallas as pl
from jax.experimental.pallas import tpu as pltpu
from jax.sharding import PartitionSpec as P

SPEED = 20.0
DAMP = 0.05
SCALE = SPEED / 3.0
SHARE = 1.0 / 3.0


def roll_lanes(value, amount):
    return value if amount % 128 == 0 else pltpu.roll(value, amount % 128, 1)


def roll_rows(value, amount):
    return value if amount % 8 == 0 else pltpu.roll(value, amount % 8, 0)


def lane_index():
    return lax.broadcasted_iota(jnp.int32, (8, 128), 1)


def row_index():
    return lax.broadcasted_iota(jnp.int32, (8, 128), 0)


def swap_bit(tiles, bit, width):
    shape = tiles[0].shape
    low = (lax.broadcasted_iota(jnp.int32, shape, 1) & width) == 0
    swapped = list(tiles)
    for i in range(len(tiles)):
        if not i & bit:
            first, second = tiles[i], tiles[i | bit]
            swapped[i] = jnp.where(low, first, roll_lanes(second, width))
            swapped[i | bit] = jnp.where(low, roll_lanes(first, -width), second)
    return swapped


def primitive(flow):
    inverse = 1.0 / flow[0]
    velocity = [flow[1] * inverse, flow[2] * inverse, flow[3] * inverse]
    squared = velocity[0] * velocity[0] + velocity[1] * velocity[1] + velocity[2] * velocity[2]
    pressure = 0.4 * (flow[4] - 0.5 * flow[0] * squared)
    return inverse, velocity, squared, pressure


def flux_along(flow, velocity, pressure, direction):
    moving = velocity[direction]
    pieces = [
        flow[1 + direction],
        flow[1] * moving,
        flow[2] * moving,
        flow[3] * moving,
        (flow[4] + pressure) * moving,
    ]
    pieces[1 + direction] = pieces[1 + direction] + pressure
    return pieces


def edge_kernel(*refs):
    flow_refs, (even_ref, odd_ref) = refs[:5], refs[5:]
    swapped_by = jnp.zeros((8, 128), jnp.int32) + lax.rem(lax.axis_index("gy"), 2) == 1
    lane = lane_index()
    top = row_index() < 4
    for c in range(5):
        packed = None
        for xh in range(4):
            tile = flow_refs[c][8 * xh : 8 * xh + 8, :]
            turned = roll_lanes(tile, 16)
            for xl in range(2):
                if xl == 0:
                    chosen = jnp.where(top, turned, roll_rows(tile, 4))
                else:
                    chosen = jnp.where(top, roll_rows(turned, 4), tile)
                x = 2 * xh + xl
                chosen = roll_lanes(chosen, 16 * x)
                packed = chosen if packed is None else jnp.where(lane >= 16 * x, chosen, packed)
        turned = jnp.where(swapped_by, roll_rows(packed, 4), packed)
        odd_ref[4 * c : 4 * c + 4, :] = turned[0:4]
        even_ref[4 * c : 4 * c + 4, :] = turned[4:8]


def pack_kernel(*refs):
    flow_refs, out_ref = refs[:5], refs[5]
    lane = lane_index()
    row = row_index()
    depth = row & 3
    both = [[None] * 8 for _ in range(5)]
    for xh in range(4):
        flow = []
        for c in range(5):
            flow.append(flow_refs[c][8 * xh : 8 * xh + 8, :])
        _, velocity, _, pressure = primitive(flow)
        along_y = flux_along(flow, velocity, pressure, 1)
        along_z = flux_along(flow, velocity, pressure, 2)
        for c in range(5):
            q, y, z = flow[c], along_y[c], along_z[c]
            far = jnp.where(lane < 2, 0.0, -DAMP * q)
            plus = roll_lanes(jnp.where(lane == 0, 0.0, -SPEED * y + 4.0 * DAMP * q), -1)
            minus_1 = roll_lanes(jnp.where(lane == 127, 0.0, SPEED * y + 4.0 * DAMP * q), 1)
            plus = plus + roll_lanes(far, -2)
            minus_1 = minus_1 + roll_lanes(jnp.where(lane >= 126, 0.0, -DAMP * q), 2)
            z_plus = jnp.where(depth == 3, roll_rows(z, 3), roll_rows(z, -1))
            z_minus = jnp.where(depth == 0, roll_rows(z, -3), roll_rows(z, 1))
            partial = (plus + minus_1) - SPEED * (z_plus - z_minus) - 6.0 * DAMP * q
            both[c][2 * xh] = jnp.where(row < 4, q, roll_rows(partial, 4))
            both[c][2 * xh + 1] = jnp.where(row < 4, roll_rows(q, 4), partial)
    for c in range(5):
        tiles = swap_bit(swap_bit(swap_bit(both[c], 4, 64), 2, 32), 1, 16)
        for g in range(8):
            out_ref[pl.ds(g * 10 + c, 4, stride=80), :] = tiles[g][0:4]
            out_ref[pl.ds(g * 10 + 5 + c, 4, stride=80), :] = tiles[g][4:8]


def border_kernel(packed_ref, even_ref, odd_ref, out_ref):
    by_odd = jnp.zeros((8, 128), jnp.int32) + lax.rem(lax.axis_index("gy"), 2) == 1
    place = lane_index() & 15
    top = row_index() < 4
    distance = jnp.where(top, 15 - place, place)
    nearest = distance == 0
    next_two = distance < 2
    sign = jnp.where(top, SPEED, -SPEED)
    flow = []
    for c in range(5):
        beyond = [ref[4 * c : 4 * c + 4, :] for ref in (even_ref, odd_ref)]
        beyond = jnp.concatenate(beyond, axis=0)
        flow.append(jnp.where(by_odd, roll_rows(beyond, 4), beyond))
    _, velocity, _, pressure = primitive(flow)
    along_y = flux_along(flow, velocity, pressure, 1)
    for c in range(5):
        first = jnp.where(nearest, sign * along_y[c] + 4.0 * DAMP * flow[c], 0.0)
        second = jnp.where(next_two, -DAMP * flow[c], 0.0)
        total = jnp.where(
            top,
            roll_lanes(first, -15) + roll_lanes(second, -14),
            roll_lanes(first, 15) + roll_lanes(second, 14),
        )
        for j, g in ((0, 0), (1, 7)):
            rows = pl.ds(g * 10 + 5 + c, 4, stride=80)
            out_ref[rows, :] = packed_ref[rows, :] + total[4 * j : 4 * j + 4]


def swapped_halves(value):
    return roll_rows(value, 4)


def in_top(top, bottom):
    return jnp.where(row_index() < 4, top, bottom)


def half_before(value, periodic=False):
    turned = roll_lanes(value, 16)
    carried = roll_rows(turned, 5)
    if periodic:
        carried = jnp.where(row_index() == 0, roll_rows(turned, 1), carried)
    earlier = jnp.where(lane_index() < 16, carried, roll_rows(turned, 4))
    return in_top(earlier, roll_rows(value, 4))


def half_after(value, periodic=False):
    turned = roll_lanes(value, -16)
    carried = roll_rows(turned, 3)
    if periodic:
        carried = jnp.where(row_index() == 7, roll_rows(turned, 7), carried)
    later = jnp.where(lane_index() >= 112, carried, roll_rows(turned, 4))
    return in_top(roll_rows(value, 4), later)


def blocks_before(value, stride):
    if stride >= 8:
        return roll_rows(value, stride // 8)
    turned = roll_lanes(value, 16 * stride)
    return jnp.where(lane_index() < 16 * stride, roll_rows(turned, 1), turned)


def blocks_after(value, stride):
    if stride >= 8:
        return roll_rows(value, -(stride // 8))
    turned = roll_lanes(value, -16 * stride)
    return jnp.where(lane_index() >= 128 - 16 * stride, roll_rows(turned, -1), turned)


def jacobian_entries(flow):
    inverse, velocity, squared, pressure = primitive(flow)
    u, v, w = velocity
    f = 0.2 * squared
    h = (flow[4] + pressure) * inverse
    return [
        [None, 1.0, None, None, None],
        [f - u * u, 1.6 * u, -0.4 * v, -0.4 * w, 0.4],
        [-u * v, v, u, None, None],
        [-u * w, w, None, u, None],
        [u * (f - h), h - 0.4 * u * u, -0.4 * u * v, -0.4 * u * w, 1.4 * u],
    ], velocity, pressure


def scaled_plus(table, factor, shift):
    result = []
    for i in range(5):
        entries = []
        for j in range(5):
            entry = table[i][j]
            entry = None if entry is None else factor * entry
            if i == j:
                entry = shift if entry is None else entry + shift
            entries.append(entry)
        result.append(entries)
    return result


def kept_where(mask, table):
    return [[None if e is None else jnp.where(mask, e, 0.0) for e in row] for row in table]


def multiply(former, latter):
    columns = len(latter[0])
    result = []
    for i in range(5):
        entries = []
        for j in range(columns):
            total = None
            for k in range(5):
                if former[i][k] is None or latter[k][j] is None:
                    continue
                term = former[i][k] * latter[k][j]
                total = term if total is None else total + term
            entries.append(total)
        result.append(entries)
    return result


def add_tables(first, second):
    return [
        [b if a is None else (a if b is None else a + b) for a, b in zip(x, y)]
        for x, y in zip(first, second)
    ]


def identity_minus(table):
    return [[(1.0 - table[i][j]) if i == j else -table[i][j] for j in range(5)] for i in range(5)]


def dense(table):
    return [[e if hasattr(e, "shape") else jnp.full((8, 128), e, jnp.float32) for e in row] for row in table]


def solve(matrix, source):
    rows = [list(matrix[i]) + list(source[i]) for i in range(5)]
    width = len(rows[0])
    for k in range(5):
        if k < 4:
            largest = jnp.abs(rows[k][k])
            for j in range(k + 1, 5):
                candidate = jnp.abs(rows[j][k])
                better = candidate > largest
                largest = jnp.maximum(candidate, largest)
                for m in range(k, width):
                    upper, lower = rows[k][m], rows[j][m]
                    rows[k][m] = jnp.where(better, lower, upper)
                    rows[j][m] = jnp.where(better, upper, lower)
        inverse = 1.0 / rows[k][k]
        for m in range(k + 1, width):
            rows[k][m] = rows[k][m] * inverse
        for i in range(k + 1, 5):
            factor = rows[i][k]
            for m in range(k + 1, width):
                rows[i][m] = rows[i][m] - factor * rows[k][m]
    for k in range(4, 0, -1):
        for i in range(k):
            factor = rows[i][k]
            for m in range(5, width):
                rows[i][m] = rows[i][m] - factor * rows[k][m]
    return [rows[i][5:] for i in range(5)]


def side_by_side(*tables):
    return [sum((list(t[i]) for t in tables), []) for i in range(5)]


def columns_of(table, begin, end):
    return [row[begin:end] for row in table]


def mapped(function, table):
    return [[function(e) for e in row] for row in table]


def both_halves(table):
    return mapped(lambda e: e + swapped_halves(e), table)


def minus(first, second):
    return [[a - b for a, b in zip(x, y)] for x, y in zip(first, second)]


def line_kernel(received_ref, out_ref):
    lane = lane_index()
    row = row_index()
    first_half = (row == 0) & (lane < 16)
    last_half = (row == 7) & (lane >= 112)
    straight = (row >= 4) == (lane >= 64)

    def exchanged(tile):
        return jnp.where(straight, tile, roll_lanes(swapped_halves(tile), 64))

    def load(position):
        tiles = []
        for u in range(4):
            halves = [
                received_ref[pl.ds((u + 4 * j) * 10 + position, 4, stride=80), :] for j in range(2)
            ]
            tiles.append(exchanged(jnp.concatenate(halves, axis=0)))
        return swap_bit(swap_bit(tiles, 2, 32), 1, 16)

    flow = [load(c) for c in range(5)]
    partial = [load(5 + c) for c in range(5)]
    cells = {t: [flow[c][t] for c in range(5)] for t in range(4)}
    cells[-2] = [half_before(e, True) for e in cells[2]]
    cells[-1] = [half_before(e, True) for e in cells[3]]
    cells[4] = [half_after(e, True) for e in cells[0]]
    cells[5] = [half_after(e, True) for e in cells[1]]
    from_before, from_after, along_x = {}, {}, {}
    for t in range(-2, 5):
        table, velocity, pressure = jacobian_entries(cells[t])
        from_before[t] = scaled_plus(table, SCALE, SHARE)
        from_after[t] = scaled_plus(table, -SCALE, SHARE)
        along_x[t] = flux_along(cells[t], velocity, pressure, 0)
    from_before[-1] = kept_where(jnp.logical_not(first_half), from_before[-1])
    from_after[4] = kept_where(jnp.logical_not(last_half), from_after[4])
    right = {}
    for t in range(4):
        right[t] = []
        for c in range(5):
            fourth = (
                (cells[t + 2][c] + cells[t - 2][c])
                - 4.0 * (cells[t + 1][c] + cells[t - 1][c])
                + 6.0 * cells[t][c]
            )
            total = partial[c][t] - SPEED * (along_x[t + 1][c] - along_x[t - 1][c]) - DAMP * fourth
            right[t].append([total * SHARE])
    right[-1] = mapped(half_before, right[3])

    def eliminated(t):
        matrix = identity_minus(
            add_tables(
                multiply(from_after[t + 1], from_before[t]),
                multiply(from_before[t - 1], from_after[t]),
            )
        )
        before = dense(multiply(from_before[t - 1], from_before[t - 2]))
        after = dense(multiply(from_after[t + 1], from_after[t + 2]))
        value = add_tables(
            right[t],
            add_tables(
                multiply(from_after[t + 1], right[t + 1]), multiply(from_before[t - 1], right[t - 1])
            ),
        )
        return matrix, before, after, value

    matrix, before, after, value = eliminated(2)
    solved = solve(matrix, side_by_side(before, after, value))
    fine_before, fine_after, fine_value = (
        columns_of(solved, 0, 5), columns_of(solved, 5, 10), columns_of(solved, 10, 11)
    )
    matrix, before, after, value = eliminated(0)
    matrix = minus(
        matrix,
        add_tables(
            multiply(after, fine_before), multiply(before, mapped(half_before, fine_after))
        ),
    )
    value = add_tables(
        value,
        add_tables(multiply(after, fine_value), multiply(before, mapped(half_before, fine_value))),
    )
    before = multiply(before, mapped(half_before, fine_before))
    after = multiply(after, fine_after)

    def pick(table, function):
        return mapped(lambda e: function(e, swapped_halves(e)), table)

    packed = [[in_top(a, swapped_halves(b)) for a, b in zip(x, y)] for x, y in zip(before, after)]
    second = [[in_top(swapped_halves(a), b) for a, b in zip(x, y)] for x, y in zip(before, after)]
    second_matrix = pick(matrix, lambda e, swapped: in_top(swapped, e))
    second_value = pick(value, lambda e, swapped: in_top(swapped, e))
    matrix = pick(matrix, in_top)
    value = pick(value, in_top)
    solved = solve(second_matrix, side_by_side(second, second_value))
    second, second_value = columns_of(solved, 0, 5), columns_of(solved, 5, 6)

    def top_before(table):
        return mapped(lambda e: in_top(blocks_before(e, 1), e), table)

    matrix = minus(matrix, both_halves(multiply(packed, mapped(half_before, second))))
    value = add_tables(value, both_halves(multiply(packed, top_before(second_value))))
    packed = multiply(packed, top_before(second))
    solved = solve(matrix, side_by_side(packed, value))
    packed, value = columns_of(solved, 0, 5), columns_of(solved, 5, 6)

    stride = 1
    while stride < 32:
        earlier = lambda table: mapped(lambda e: blocks_before(e, stride), table)
        later = lambda table: mapped(lambda e: blocks_after(e, stride), table)
        towards = lambda x, y: [[in_top(a, b) for a, b in zip(p, q)] for p, q in zip(x, y)]
        prior, following = earlier(packed), later(packed)
        crossed = mapped(swapped_halves, towards(following, prior))
        matrix = identity_minus(both_halves(multiply(packed, crossed)))
        beside = towards(earlier(value), later(value))
        value = add_tables(value, both_halves(multiply(packed, beside)))
        if stride < 16:
            packed = multiply(packed, towards(prior, following))
            solved = solve(matrix, side_by_side(packed, value))
            packed, value = columns_of(solved, 0, 5), columns_of(solved, 5, 6)
        else:
            value = solve(matrix, value)
        stride *= 2

    last_block = ((row & 3) == 3) & (lane >= 112)
    ahead = mapped(lambda e: jnp.where(last_block, 0.0, blocks_after(e, 1)), value)
    around = [[in_top(a[0], b[0])] for a, b in zip(value, ahead)]
    middle = add_tables(second_value, both_halves(multiply(second, around)))
    result = {
        0: [[in_top(a[0], b[0])] for a, b in zip(value, middle)],
        4: [[in_top(a[0], b[0])] for a, b in zip(middle, ahead)],
    }
    result[2] = add_tables(
        fine_value, add_tables(multiply(fine_before, result[0]), multiply(fine_after, result[4]))
    )
    for t in (1, 3):
        result[t] = add_tables(
            right[t],
            add_tables(
                multiply(from_before[t - 1], result[t - 1]), multiply(from_after[t + 1], result[t + 1])
            ),
        )
    for c in range(5):
        tiles = swap_bit(swap_bit([result[t][c][0] for t in range(4)], 2, 32), 1, 16)
        for u in range(4):
            tile = exchanged(tiles[u])
            for j in range(2):
                out_ref[pl.ds((u + 4 * j) * 5 + c, 4, stride=40), :] = tile[4 * j : 4 * j + 4]


def unpack_kernel(returned_ref, out_ref):
    for c in range(5):
        tiles = [returned_ref[pl.ds(g * 5 + c, 4, stride=40), :] for g in range(8)]
        tiles = swap_bit(tiles, 4, 64)
        tiles = swap_bit(tiles, 2, 32)
        tiles = swap_bit(tiles, 1, 16)
        for x in range(8):
            out_ref[c * 32 + x * 4 : c * 32 + x * 4 + 4, :] = tiles[x]


def call(kernel, rows, *operands, **options):
    whole = pl.BlockSpec(memory_space=pltpu.VMEM)
    return pl.pallas_call(
        kernel,
        out_shape=jax.ShapeDtypeStruct((rows, 128), jnp.float32),
        in_specs=[whole] * len(operands),
        out_specs=whole,
        compiler_params=pltpu.CompilerParams(vmem_limit_bytes=32 * 1024 * 1024),
        **options,
    )(*operands)


def per_device(flow_state):
    flow = [flow_state[c].reshape(32, 128) for c in range(5)]
    count = lax.axis_size("gy")
    vmem = pl.BlockSpec(memory_space=pltpu.VMEM)
    edges = pl.pallas_call(
        edge_kernel,
        out_shape=[jax.ShapeDtypeStruct((20, 128), jnp.float32)] * 2,
        in_specs=[vmem] * 5,
        out_specs=[vmem] * 2,
        compiler_params=pltpu.CompilerParams(vmem_limit_bytes=32 * 1024 * 1024),
    )(*flow)
    exchanges = [None, None]
    for start in (0, 1):
        pairs = [((start + i) % count, (start + i + 1) % count) for i in range(0, count, 2)]
        exchanges[start] = lax.ppermute(edges[1 - start], "gy", pairs + [(b, a) for a, b in pairs])
    cost = pl.CostEstimate(flops=4000000, bytes_accessed=250000, transcendentals=0)
    packed = call(pack_kernel, 320, *flow, cost_estimate=cost)
    packed = call(border_kernel, 320, packed, *exchanges[::-1], input_output_aliases={0: 0})
    received = lax.all_to_all(
        packed.reshape(32, 1, 1280), "gx", split_axis=0, concat_axis=0, tiled=True
    ).reshape(320, 128)
    solved = call(line_kernel, 160, received)
    returned = lax.all_to_all(
        solved.reshape(32, 1, 640), "gx", split_axis=0, concat_axis=0, tiled=True
    ).reshape(160, 128)
    return call(unpack_kernel, 160, returned).reshape(flow_state.shape)


def solution(mesh):
    placed = (P(None, "gx", None, "gy"),)
    return jax.shard_map(
        per_device, mesh=mesh, in_specs=placed, out_specs=P(None, "gx", None, "gy"), check_vma=False
    )
```

```python
import jax
import jax.numpy as jnp
from jax import lax
from jax.experimental import pallas as pl
from jax.experimental.pallas import tpu as pltpu
from jax.sharding import PartitionSpec as P

SPEED = 20.0
DAMP = 0.05
SCALE = SPEED / 3.0
SHARE = 1.0 / 3.0


def roll_lanes(value, amount):
    return value if amount % 128 == 0 else pltpu.roll(value, amount % 128, 1)


def roll_rows(value, amount):
    return value if amount % 8 == 0 else pltpu.roll(value, amount % 8, 0)


def lane_index():
    return lax.broadcasted_iota(jnp.int32, (8, 128), 1)


def row_index():
    return lax.broadcasted_iota(jnp.int32, (8, 128), 0)


def swap_bit(tiles, bit, width):
    shape = tiles[0].shape
    low = (lax.broadcasted_iota(jnp.int32, shape, 1) & width) == 0
    swapped = list(tiles)
    for i in range(len(tiles)):
        if not i & bit:
            first, second = tiles[i], tiles[i | bit]
            swapped[i] = jnp.where(low, first, roll_lanes(second, width))
            swapped[i | bit] = jnp.where(low, roll_lanes(first, -width), second)
    return swapped


def primitive(flow):
    inverse = 1.0 / flow[0]
    velocity = [flow[1] * inverse, flow[2] * inverse, flow[3] * inverse]
    squared = velocity[0] * velocity[0] + velocity[1] * velocity[1] + velocity[2] * velocity[2]
    pressure = 0.4 * (flow[4] - 0.5 * flow[0] * squared)
    return inverse, velocity, squared, pressure


def flux_along(flow, velocity, pressure, direction):
    moving = velocity[direction]
    pieces = [
        flow[1 + direction],
        flow[1] * moving,
        flow[2] * moving,
        flow[3] * moving,
        (flow[4] + pressure) * moving,
    ]
    pieces[1 + direction] = pieces[1 + direction] + pressure
    return pieces


def edge_kernel(*refs):
    flow_refs, (odd_ref, even_ref) = refs[:5], refs[5:]
    swapped_by = jnp.zeros((8, 128), jnp.int32) + lax.rem(lax.axis_index("gy"), 2) == 1
    lane = lane_index()
    top = row_index() < 4
    for c in range(5):
        packed = None
        for xh in range(4):
            tile = flow_refs[c][8 * xh : 8 * xh + 8, :]
            turned = roll_lanes(tile, 16)
            for xl in range(2):
                if xl == 0:
                    chosen = jnp.where(top, turned, roll_rows(tile, 4))
                else:
                    chosen = jnp.where(top, roll_rows(turned, 4), tile)
                x = 2 * xh + xl
                chosen = roll_lanes(chosen, 16 * x)
                packed = chosen if packed is None else jnp.where(lane >= 16 * x, chosen, packed)
        turned = jnp.where(swapped_by, roll_rows(packed, 4), packed)
        odd_ref[4 * c : 4 * c + 4, :] = turned[0:4]
        even_ref[4 * c : 4 * c + 4, :] = turned[4:8]


def pack_kernel(*refs):
    flow_refs, out_ref = refs[:5], refs[5]
    lane = lane_index()
    row = row_index()
    depth = row & 3
    both = [[None] * 8 for _ in range(5)]
    for xh in range(4):
        flow = []
        for c in range(5):
            flow.append(flow_refs[c][8 * xh : 8 * xh + 8, :])
        _, velocity, _, pressure = primitive(flow)
        along_y = flux_along(flow, velocity, pressure, 1)
        along_z = flux_along(flow, velocity, pressure, 2)
        for c in range(5):
            q, y, z = flow[c], along_y[c], along_z[c]
            far = jnp.where(lane < 2, 0.0, -DAMP * q)
            plus = roll_lanes(jnp.where(lane == 0, 0.0, -SPEED * y + 4.0 * DAMP * q), -1)
            minus_1 = roll_lanes(jnp.where(lane == 127, 0.0, SPEED * y + 4.0 * DAMP * q), 1)
            plus = plus + roll_lanes(far, -2)
            minus_1 = minus_1 + roll_lanes(jnp.where(lane >= 126, 0.0, -DAMP * q), 2)
            z_plus = jnp.where(depth == 3, roll_rows(z, 3), roll_rows(z, -1))
            z_minus = jnp.where(depth == 0, roll_rows(z, -3), roll_rows(z, 1))
            partial = (plus + minus_1) - SPEED * (z_plus - z_minus) - 6.0 * DAMP * q
            both[c][2 * xh] = jnp.where(row < 4, q, roll_rows(partial, 4))
            both[c][2 * xh + 1] = jnp.where(row < 4, roll_rows(q, 4), partial)
    for c in range(5):
        tiles = swap_bit(swap_bit(swap_bit(both[c], 4, 64), 2, 32), 1, 16)
        for g in range(8):
            out_ref[pl.ds(g * 10 + c, 4, stride=80), :] = tiles[g][0:4]
            out_ref[pl.ds(g * 10 + 5 + c, 4, stride=80), :] = tiles[g][4:8]


def border_kernel(packed_ref, odd_ref, even_ref, out_ref):
    by_odd = jnp.zeros((8, 128), jnp.int32) + lax.rem(lax.axis_index("gy"), 2) == 1
    place = lane_index() & 15
    top = row_index() < 4
    distance = jnp.where(top, 15 - place, place)
    nearest = distance == 0
    next_two = distance < 2
    sign = jnp.where(top, SPEED, -SPEED)
    flow = []
    for c in range(5):
        beyond = [ref[4 * c : 4 * c + 4, :] for ref in (even_ref, odd_ref)]
        beyond = jnp.concatenate(beyond, axis=0)
        flow.append(jnp.where(by_odd, roll_rows(beyond, 4), beyond))
    _, velocity, _, pressure = primitive(flow)
    along_y = flux_along(flow, velocity, pressure, 1)
    for c in range(5):
        first = jnp.where(nearest, sign * along_y[c] + 4.0 * DAMP * flow[c], 0.0)
        second = jnp.where(next_two, -DAMP * flow[c], 0.0)
        total = jnp.where(
            top,
            roll_lanes(first, -15) + roll_lanes(second, -14),
            roll_lanes(first, 15) + roll_lanes(second, 14),
        )
        for j, g in ((0, 0), (1, 7)):
            rows = pl.ds(g * 10 + 5 + c, 4, stride=80)
            out_ref[rows, :] = packed_ref[rows, :] + total[4 * j : 4 * j + 4]


def swapped_halves(value):
    return roll_rows(value, 4)


def in_top(top, bottom):
    return jnp.where(row_index() < 4, top, bottom)


def half_before(value, periodic=False):
    turned = roll_lanes(value, 16)
    carried = roll_rows(turned, 5)
    if periodic:
        carried = jnp.where(row_index() == 0, roll_rows(turned, 1), carried)
    earlier = jnp.where(lane_index() < 16, carried, roll_rows(turned, 4))
    return in_top(earlier, roll_rows(value, 4))


def half_after(value, periodic=False):
    turned = roll_lanes(value, -16)
    carried = roll_rows(turned, 3)
    if periodic:
        carried = jnp.where(row_index() == 7, roll_rows(turned, 7), carried)
    later = jnp.where(lane_index() >= 112, carried, roll_rows(turned, 4))
    return in_top(roll_rows(value, 4), later)


def blocks_before(value, stride):
    if stride >= 8:
        return roll_rows(value, stride // 8)
    turned = roll_lanes(value, 16 * stride)
    return jnp.where(lane_index() < 16 * stride, roll_rows(turned, 1), turned)


def blocks_after(value, stride):
    if stride >= 8:
        return roll_rows(value, -(stride // 8))
    turned = roll_lanes(value, -16 * stride)
    return jnp.where(lane_index() >= 128 - 16 * stride, roll_rows(turned, -1), turned)


def jacobian_entries(flow):
    inverse, velocity, squared, pressure = primitive(flow)
    u, v, w = velocity
    f = 0.2 * squared
    h = (flow[4] + pressure) * inverse
    return [
        [None, 1.0, None, None, None],
        [f - u * u, 1.6 * u, -0.4 * v, -0.4 * w, 0.4],
        [-u * v, v, u, None, None],
        [-u * w, w, None, u, None],
        [u * (f - h), h - 0.4 * u * u, -0.4 * u * v, -0.4 * u * w, 1.4 * u],
    ], velocity, pressure


def scaled_plus(table, factor, shift):
    result = []
    for i in range(5):
        entries = []
        for j in range(5):
            entry = table[i][j]
            entry = None if entry is None else factor * entry
            if i == j:
                entry = shift if entry is None else entry + shift
            entries.append(entry)
        result.append(entries)
    return result


def kept_where(mask, table):
    return [[None if e is None else jnp.where(mask, e, 0.0) for e in row] for row in table]


def multiply(former, latter):
    columns = len(latter[0])
    result = []
    for i in range(5):
        entries = []
        for j in range(columns):
            total = None
            for k in range(5):
                if former[i][k] is None or latter[k][j] is None:
                    continue
                term = former[i][k] * latter[k][j]
                total = term if total is None else total + term
            entries.append(total)
        result.append(entries)
    return result


def add_tables(first, second):
    return [
        [b if a is None else (a if b is None else a + b) for a, b in zip(x, y)]
        for x, y in zip(first, second)
    ]


def identity_minus(table):
    return [[(1.0 - table[i][j]) if i == j else -table[i][j] for j in range(5)] for i in range(5)]


def minus_identity(table):
    return [[(table[i][j] - 1.0) if i == j else table[i][j] for j in range(5)] for i in range(5)]


def dense(table):
    return [[e if hasattr(e, "shape") else jnp.full((8, 128), e, jnp.float32) for e in row] for row in table]


def solve(matrix, source):
    rows = [list(matrix[i]) + list(source[i]) for i in range(5)]
    width = len(rows[0])
    for k in range(5):
        if k < 4:
            largest = jnp.abs(rows[k][k])
            for j in range(k + 1, 5):
                candidate = jnp.abs(rows[j][k])
                better = candidate > largest
                largest = jnp.maximum(candidate, largest)
                for m in range(k, width):
                    upper, lower = rows[k][m], rows[j][m]
                    rows[k][m] = jnp.where(better, lower, upper)
                    rows[j][m] = jnp.where(better, upper, lower)
        inverse = 1.0 / rows[k][k]
        for m in range(k + 1, width):
            rows[k][m] = rows[k][m] * inverse
        for i in range(k + 1, 5):
            factor = rows[i][k]
            for m in range(k + 1, width):
                rows[i][m] = rows[i][m] - factor * rows[k][m]
    for k in range(4, 0, -1):
        for i in range(k):
            factor = rows[i][k]
            for m in range(5, width):
                rows[i][m] = rows[i][m] - factor * rows[k][m]
    return [rows[i][5:] for i in range(5)]


def side_by_side(*tables):
    return [sum((list(t[i]) for t in tables), []) for i in range(5)]


def columns_of(table, begin, end):
    return [row[begin:end] for row in table]


def mapped(function, table):
    return [[function(e) for e in row] for row in table]


def both_halves(table):
    return mapped(lambda e: e + swapped_halves(e), table)


def minus(first, second):
    return [[a - b for a, b in zip(x, y)] for x, y in zip(first, second)]


def line_kernel(received_ref, out_ref):
    lane = lane_index()
    row = row_index()
    first_half = (row == 0) & (lane < 16)
    last_half = (row == 7) & (lane >= 112)
    straight = (row >= 4) == (lane >= 64)

    def exchanged(tile):
        return jnp.where(straight, tile, roll_lanes(swapped_halves(tile), 64))

    def load(position):
        tiles = []
        for u in range(4):
            halves = [
                received_ref[pl.ds((u + 4 * j) * 10 + position, 4, stride=80), :] for j in range(2)
            ]
            tiles.append(exchanged(jnp.concatenate(halves, axis=0)))
        return swap_bit(swap_bit(tiles, 2, 32), 1, 16)

    flow = [load(c) for c in range(5)]
    partial = [load(5 + c) for c in range(5)]
    cells = {t: [flow[c][t] for c in range(5)] for t in range(4)}
    cells[-2] = [half_before(e, True) for e in cells[2]]
    cells[-1] = [half_before(e, True) for e in cells[3]]
    cells[4] = [half_after(e, True) for e in cells[0]]
    cells[5] = [half_after(e, True) for e in cells[1]]
    from_before, from_after, along_x, tables = {}, {}, {}, {}
    for t in range(-2, 5):
        table, velocity, pressure = jacobian_entries(cells[t])
        tables[t] = [[None if e is None else SCALE * e for e in x] for x in table]
        from_before[t] = scaled_plus(table, SCALE, SHARE)
        from_after[t] = scaled_plus(table, -SCALE, SHARE)
        along_x[t] = flux_along(cells[t], velocity, pressure, 0)
    from_before[-1] = kept_where(jnp.logical_not(first_half), from_before[-1])
    from_after[4] = kept_where(jnp.logical_not(last_half), from_after[4])
    right = {}
    for t in range(4):
        right[t] = []
        for c in range(5):
            fourth = (
                (cells[t + 2][c] + cells[t - 2][c])
                - 4.0 * (cells[t + 1][c] + cells[t - 1][c])
                + 6.0 * cells[t][c]
            )
            total = partial[c][t] - SPEED * (along_x[t + 1][c] - along_x[t - 1][c]) - DAMP * fourth
            right[t].append([total * SHARE])
    right[-1] = mapped(half_before, right[3])

    def eliminated(t):
        if t == 2:
            outer, inner = tables[t + 1], tables[t - 1]
            matrix = multiply(add_tables(outer, inner), tables[t])
            for i in range(5):
                for j in range(5):
                    if outer[i][j] is not None:
                        change = SHARE * (outer[i][j] - inner[i][j])
                        matrix[i][j] = change if matrix[i][j] is None else matrix[i][j] + change
                matrix[i][i] = matrix[i][i] + (1.0 - 2.0 * SHARE * SHARE)
        else:
            matrix = identity_minus(
                add_tables(
                    multiply(from_after[t + 1], from_before[t]),
                    multiply(from_before[t - 1], from_after[t]),
                )
            )
        before = dense(multiply(from_before[t - 1], from_before[t - 2]))
        after = dense(multiply(from_after[t + 1], from_after[t + 2]))
        value = add_tables(
            right[t],
            add_tables(
                multiply(from_after[t + 1], right[t + 1]), multiply(from_before[t - 1], right[t - 1])
            ),
        )
        return matrix, before, after, value

    matrix, before, after, value = eliminated(2)
    solved = solve(matrix, side_by_side(before, after, value))
    fine_before, fine_after, fine_value = (
        columns_of(solved, 0, 5), columns_of(solved, 5, 10), columns_of(solved, 10, 11)
    )
    matrix, before, after, value = eliminated(0)
    matrix = minus(
        matrix,
        add_tables(
            multiply(after, fine_before), multiply(before, mapped(half_before, fine_after))
        ),
    )
    value = add_tables(
        value,
        add_tables(multiply(after, fine_value), multiply(before, mapped(half_before, fine_value))),
    )
    before = multiply(before, mapped(half_before, fine_before))
    after = multiply(after, fine_after)

    def pick(table, function):
        return mapped(lambda e: function(e, swapped_halves(e)), table)

    packed = [[in_top(a, swapped_halves(b)) for a, b in zip(x, y)] for x, y in zip(before, after)]
    second = [[in_top(swapped_halves(a), b) for a, b in zip(x, y)] for x, y in zip(before, after)]
    second_matrix = pick(matrix, lambda e, swapped: in_top(swapped, e))
    second_value = pick(value, lambda e, swapped: in_top(swapped, e))
    matrix = pick(matrix, in_top)
    value = pick(value, in_top)
    solved = solve(second_matrix, side_by_side(second, second_value))
    second, second_value = columns_of(solved, 0, 5), columns_of(solved, 5, 6)

    def top_before(table):
        return mapped(lambda e: in_top(blocks_before(e, 1), e), table)

    matrix = minus(matrix, both_halves(multiply(packed, mapped(half_before, second))))
    value = add_tables(value, both_halves(multiply(packed, top_before(second_value))))
    packed = multiply(packed, top_before(second))
    solved = solve(matrix, side_by_side(packed, value))
    packed, value = columns_of(solved, 0, 5), columns_of(solved, 5, 6)

    stride = 1
    while stride < 32:
        earlier = lambda table: mapped(lambda e: blocks_before(e, stride), table)
        later = lambda table: mapped(lambda e: blocks_after(e, stride), table)
        towards = lambda x, y: [[in_top(a, b) for a, b in zip(p, q)] for p, q in zip(x, y)]
        prior, following = earlier(packed), later(packed)
        crossed = mapped(swapped_halves, towards(following, prior))
        matrix = minus_identity(both_halves(multiply(packed, crossed)))
        beside = towards(earlier(value), later(value))
        moved = both_halves(multiply(packed, beside))
        value = add_tables(moved, value) if stride == 1 else minus(moved, value)
        if stride < 16:
            packed = multiply(packed, towards(prior, following))
            solved = solve(matrix, side_by_side(packed, value))
            packed, value = columns_of(solved, 0, 5), columns_of(solved, 5, 6)
        else:
            value = solve(matrix, value)
        stride *= 2

    value = mapped(lambda e: -e, value)
    last_block = ((row & 3) == 3) & (lane >= 112)
    ahead = mapped(lambda e: jnp.where(last_block, 0.0, blocks_after(e, 1)), value)
    around = [[in_top(a[0], b[0])] for a, b in zip(value, ahead)]
    middle = add_tables(second_value, both_halves(multiply(second, around)))
    result = {
        0: [[in_top(a[0], b[0])] for a, b in zip(value, middle)],
        4: [[in_top(a[0], b[0])] for a, b in zip(middle, ahead)],
    }
    result[2] = add_tables(
        fine_value, add_tables(multiply(fine_before, result[0]), multiply(fine_after, result[4]))
    )
    for t in (1, 3):
        result[t] = add_tables(
            right[t],
            add_tables(
                multiply(from_before[t - 1], result[t - 1]), multiply(from_after[t + 1], result[t + 1])
            ),
        )
    for c in range(5):
        tiles = swap_bit(swap_bit([result[t][c][0] for t in range(4)], 2, 32), 1, 16)
        for u in range(4):
            tile = exchanged(tiles[u])
            for j in range(2):
                out_ref[pl.ds((u + 4 * j) * 5 + c, 4, stride=40), :] = tile[4 * j : 4 * j + 4]


def unpack_kernel(returned_ref, out_ref):
    for c in range(5):
        tiles = [returned_ref[pl.ds(g * 5 + c, 4, stride=40), :] for g in range(8)]
        tiles = swap_bit(tiles, 4, 64)
        tiles = swap_bit(tiles, 2, 32)
        tiles = swap_bit(tiles, 1, 16)
        for x in range(8):
            out_ref[c * 32 + x * 4 : c * 32 + x * 4 + 4, :] = tiles[x]


def call(kernel, rows, *operands, **options):
    whole = pl.BlockSpec(memory_space=pltpu.VMEM)
    return pl.pallas_call(
        kernel,
        out_shape=jax.ShapeDtypeStruct((rows, 128), jnp.float32),
        in_specs=[whole] * len(operands),
        out_specs=whole,
        compiler_params=pltpu.CompilerParams(vmem_limit_bytes=32 * 1024 * 1024),
        **options,
    )(*operands)


def per_device(flow_state):
    flow = [flow_state[c].reshape(32, 128) for c in range(5)]
    count = lax.axis_size("gy")
    vmem = pl.BlockSpec(memory_space=pltpu.VMEM)
    edges = pl.pallas_call(
        edge_kernel,
        out_shape=[jax.ShapeDtypeStruct((20, 128), jnp.float32)] * 2,
        in_specs=[vmem] * 5,
        out_specs=[vmem] * 2,
        compiler_params=pltpu.CompilerParams(vmem_limit_bytes=32 * 1024 * 1024),
    )(*flow)
    exchanges = [None, None]
    for start in (1, 0):
        pairs = [((start + i) % count, (start + i + 1) % count) for i in range(0, count, 2)]
        exchanges[start] = lax.ppermute(edges[start], "gy", pairs + [(b, a) for a, b in pairs])
    cost = pl.CostEstimate(flops=4000000, bytes_accessed=250000, transcendentals=0)
    packed = call(pack_kernel, 320, *flow, cost_estimate=cost)
    packed = call(border_kernel, 320, packed, *exchanges, input_output_aliases={0: 0})
    received = lax.all_to_all(
        packed.reshape(32, 1, 1280), "gx", split_axis=0, concat_axis=0, tiled=True
    ).reshape(320, 128)
    solved = call(line_kernel, 160, received)
    returned = lax.all_to_all(
        solved.reshape(32, 1, 640), "gx", split_axis=0, concat_axis=0, tiled=True
    ).reshape(160, 128)
    return call(unpack_kernel, 160, returned).reshape(flow_state.shape)


def solution(mesh):
    placed = (P(None, "gx", None, "gy"),)
    return jax.shard_map(
        per_device, mesh=mesh, in_specs=placed, out_specs=P(None, "gx", None, "gy"), check_vma=False
    )
```

```python
import jax
import jax.numpy as jnp
from jax import lax
from jax.experimental import pallas as pl
from jax.experimental.pallas import tpu as pltpu
from jax.sharding import PartitionSpec as P

SPEED = 20.0
DAMP = 0.05
SCALE = SPEED / 3.0
SHARE = 1.0 / 3.0


def roll_lanes(value, amount):
    return value if amount % 128 == 0 else pltpu.roll(value, amount % 128, 1)


def roll_rows(value, amount):
    return value if amount % 8 == 0 else pltpu.roll(value, amount % 8, 0)


def lane_index():
    return lax.broadcasted_iota(jnp.int32, (8, 128), 1)


def row_index():
    return lax.broadcasted_iota(jnp.int32, (8, 128), 0)


def swap_bit(tiles, bit, width):
    shape = tiles[0].shape
    low = (lax.broadcasted_iota(jnp.int32, shape, 1) & width) == 0
    swapped = list(tiles)
    for i in range(len(tiles)):
        if not i & bit:
            first, second = tiles[i], tiles[i | bit]
            swapped[i] = jnp.where(low, first, roll_lanes(second, width))
            swapped[i | bit] = jnp.where(low, roll_lanes(first, -width), second)
    return swapped


def primitive(flow):
    inverse = 1.0 / flow[0]
    velocity = [flow[1] * inverse, flow[2] * inverse, flow[3] * inverse]
    squared = velocity[0] * velocity[0] + velocity[1] * velocity[1] + velocity[2] * velocity[2]
    pressure = 0.4 * (flow[4] - 0.5 * flow[0] * squared)
    return inverse, velocity, squared, pressure


def flux_along(flow, velocity, pressure, direction):
    moving = velocity[direction]
    pieces = [
        flow[1 + direction],
        flow[1] * moving,
        flow[2] * moving,
        flow[3] * moving,
        (flow[4] + pressure) * moving,
    ]
    pieces[1 + direction] = pieces[1 + direction] + pressure
    return pieces


def edge_kernel(*refs):
    flow_refs, (odd_ref, even_ref) = refs[:5], refs[5:]
    swapped_by = jnp.zeros((8, 128), jnp.int32) + lax.rem(lax.axis_index("gy"), 2) == 1
    lane = lane_index()
    top = row_index() < 4
    for c in range(5):
        packed = None
        for xh in range(4):
            tile = flow_refs[c][8 * xh : 8 * xh + 8, :]
            turned = roll_lanes(tile, 16)
            for xl in range(2):
                if xl == 0:
                    chosen = jnp.where(top, turned, roll_rows(tile, 4))
                else:
                    chosen = jnp.where(top, roll_rows(turned, 4), tile)
                x = 2 * xh + xl
                chosen = roll_lanes(chosen, 16 * x)
                packed = chosen if packed is None else jnp.where(lane >= 16 * x, chosen, packed)
        turned = jnp.where(swapped_by, roll_rows(packed, 4), packed)
        odd_ref[4 * c : 4 * c + 4, :] = turned[0:4]
        even_ref[4 * c : 4 * c + 4, :] = turned[4:8]


def pack_kernel(*refs):
    flow_refs, out_ref = refs[:5], refs[5]
    lane = lane_index()
    row = row_index()
    depth = row & 3
    both = [[None] * 8 for _ in range(5)]
    for xh in range(4):
        flow = []
        for c in range(5):
            flow.append(flow_refs[c][8 * xh : 8 * xh + 8, :])
        _, velocity, _, pressure = primitive(flow)
        along_y = flux_along(flow, velocity, pressure, 1)
        along_z = flux_along(flow, velocity, pressure, 2)
        for c in range(5):
            q, y, z = flow[c], along_y[c], along_z[c]
            far = jnp.where(lane < 2, 0.0, -DAMP * q)
            plus = roll_lanes(jnp.where(lane == 0, 0.0, -SPEED * y + 4.0 * DAMP * q), -1)
            minus_1 = roll_lanes(jnp.where(lane == 127, 0.0, SPEED * y + 4.0 * DAMP * q), 1)
            plus = plus + roll_lanes(far, -2)
            minus_1 = minus_1 + roll_lanes(jnp.where(lane >= 126, 0.0, -DAMP * q), 2)
            z_plus = jnp.where(depth == 3, roll_rows(z, 3), roll_rows(z, -1))
            z_minus = jnp.where(depth == 0, roll_rows(z, -3), roll_rows(z, 1))
            partial = (plus + minus_1) - SPEED * (z_plus - z_minus) - 6.0 * DAMP * q
            both[c][2 * xh] = jnp.where(row < 4, q, roll_rows(partial, 4))
            both[c][2 * xh + 1] = jnp.where(row < 4, roll_rows(q, 4), partial)
    for c in range(5):
        tiles = swap_bit(swap_bit(swap_bit(both[c], 4, 64), 2, 32), 1, 16)
        for g in range(8):
            out_ref[pl.ds(g * 10 + c, 4, stride=80), :] = tiles[g][0:4]
            out_ref[pl.ds(g * 10 + 5 + c, 4, stride=80), :] = tiles[g][4:8]


def border_kernel(packed_ref, odd_ref, even_ref, out_ref):
    by_odd = jnp.zeros((8, 128), jnp.int32) + lax.rem(lax.axis_index("gy"), 2) == 1
    place = lane_index() & 15
    top = row_index() < 4
    distance = jnp.where(top, 15 - place, place)
    nearest = distance == 0
    next_two = distance < 2
    sign = jnp.where(top, SPEED, -SPEED)
    flow = []
    for c in range(5):
        beyond = [ref[4 * c : 4 * c + 4, :] for ref in (even_ref, odd_ref)]
        beyond = jnp.concatenate(beyond, axis=0)
        flow.append(jnp.where(by_odd, roll_rows(beyond, 4), beyond))
    _, velocity, _, pressure = primitive(flow)
    along_y = flux_along(flow, velocity, pressure, 1)
    for c in range(5):
        first = jnp.where(nearest, sign * along_y[c] + 4.0 * DAMP * flow[c], 0.0)
        second = jnp.where(next_two, -DAMP * flow[c], 0.0)
        total = jnp.where(
            top,
            roll_lanes(first, -15) + roll_lanes(second, -14),
            roll_lanes(first, 15) + roll_lanes(second, 14),
        )
        for j, g in ((0, 0), (1, 7)):
            rows = pl.ds(g * 10 + 5 + c, 4, stride=80)
            out_ref[rows, :] = packed_ref[rows, :] + total[4 * j : 4 * j + 4]


def swapped_halves(value):
    return roll_rows(value, 4)


def in_top(top, bottom):
    return jnp.where(row_index() < 4, top, bottom)


def half_before(value, periodic=False):
    turned = roll_lanes(value, 16)
    carried = roll_rows(turned, 5)
    if periodic:
        carried = jnp.where(row_index() == 0, roll_rows(turned, 1), carried)
    earlier = jnp.where(lane_index() < 16, carried, roll_rows(turned, 4))
    return in_top(earlier, roll_rows(value, 4))


def half_after(value, periodic=False):
    turned = roll_lanes(value, -16)
    carried = roll_rows(turned, 3)
    if periodic:
        carried = jnp.where(row_index() == 7, roll_rows(turned, 7), carried)
    later = jnp.where(lane_index() >= 112, carried, roll_rows(turned, 4))
    return in_top(roll_rows(value, 4), later)


def blocks_before(value, stride):
    if stride >= 8:
        return roll_rows(value, stride // 8)
    turned = roll_lanes(value, 16 * stride)
    return jnp.where(lane_index() < 16 * stride, roll_rows(turned, 1), turned)


def blocks_after(value, stride):
    if stride >= 8:
        return roll_rows(value, -(stride // 8))
    turned = roll_lanes(value, -16 * stride)
    return jnp.where(lane_index() >= 128 - 16 * stride, roll_rows(turned, -1), turned)


def jacobian_entries(flow):
    inverse, velocity, squared, pressure = primitive(flow)
    u, v, w = velocity
    f = 0.2 * squared
    h = (flow[4] + pressure) * inverse
    return [
        [None, 1.0, None, None, None],
        [f - u * u, 1.6 * u, -0.4 * v, -0.4 * w, 0.4],
        [-u * v, v, u, None, None],
        [-u * w, w, None, u, None],
        [u * (f - h), h - 0.4 * u * u, -0.4 * u * v, -0.4 * u * w, 1.4 * u],
    ], velocity, pressure


def scaled_plus(table, factor, shift):
    result = []
    for i in range(5):
        entries = []
        for j in range(5):
            entry = table[i][j]
            entry = None if entry is None else factor * entry
            if i == j:
                entry = shift if entry is None else entry + shift
            entries.append(entry)
        result.append(entries)
    return result


def kept_where(mask, table):
    return [[None if e is None else jnp.where(mask, e, 0.0) for e in row] for row in table]


def multiply(former, latter):
    columns = len(latter[0])
    result = []
    for i in range(5):
        entries = []
        for j in range(columns):
            total = None
            for k in range(5):
                if former[i][k] is None or latter[k][j] is None:
                    continue
                term = former[i][k] * latter[k][j]
                total = term if total is None else total + term
            entries.append(total)
        result.append(entries)
    return result


def add_tables(first, second):
    return [
        [b if a is None else (a if b is None else a + b) for a, b in zip(x, y)]
        for x, y in zip(first, second)
    ]


def identity_minus(table):
    return [[(1.0 - table[i][j]) if i == j else -table[i][j] for j in range(5)] for i in range(5)]


def minus_identity(table):
    return [[(table[i][j] - 1.0) if i == j else table[i][j] for j in range(5)] for i in range(5)]


def dense(table):
    return [[e if hasattr(e, "shape") else jnp.full((8, 128), e, jnp.float32) for e in row] for row in table]


def solve(matrix, source):
    rows = [list(matrix[i]) + list(source[i]) for i in range(5)]
    width = len(rows[0])
    for k in range(5):
        if k < 4:
            largest = jnp.abs(rows[k][k])
            for j in range(k + 1, 5):
                candidate = jnp.abs(rows[j][k])
                better = candidate > largest
                largest = jnp.maximum(candidate, largest)
                for m in range(k, width):
                    upper, lower = rows[k][m], rows[j][m]
                    rows[k][m] = jnp.where(better, lower, upper)
                    rows[j][m] = jnp.where(better, upper, lower)
        inverse = 1.0 / rows[k][k]
        for m in range(k + 1, width):
            rows[k][m] = rows[k][m] * inverse
        for i in range(k + 1, 5):
            factor = rows[i][k]
            for m in range(k + 1, width):
                rows[i][m] = rows[i][m] - factor * rows[k][m]
    for k in range(4, 0, -1):
        for i in range(k):
            factor = rows[i][k]
            for m in range(5, width):
                rows[i][m] = rows[i][m] - factor * rows[k][m]
    return [rows[i][5:] for i in range(5)]


def side_by_side(*tables):
    return [sum((list(t[i]) for t in tables), []) for i in range(5)]


def columns_of(table, begin, end):
    return [row[begin:end] for row in table]


def mapped(function, table):
    return [[function(e) for e in row] for row in table]


def both_halves(table):
    return mapped(lambda e: e + swapped_halves(e), table)


def minus(first, second):
    return [[a - b for a, b in zip(x, y)] for x, y in zip(first, second)]


def line_kernel(received_ref, out_ref):
    lane = lane_index()
    row = row_index()
    first_half = (row == 0) & (lane < 16)
    last_half = (row == 7) & (lane >= 112)
    straight = (row >= 4) == (lane >= 64)

    def exchanged(tile):
        return jnp.where(straight, tile, roll_lanes(swapped_halves(tile), 64))

    def load(position):
        tiles = []
        for u in range(4):
            halves = [
                received_ref[pl.ds((u + 4 * j) * 10 + position, 4, stride=80), :] for j in range(2)
            ]
            tiles.append(exchanged(jnp.concatenate(halves, axis=0)))
        return swap_bit(swap_bit(tiles, 2, 32), 1, 16)

    flow = [load(c) for c in range(5)]
    partial = [load(5 + c) for c in range(5)]
    cells = {t: [flow[c][t] for c in range(5)] for t in range(4)}
    cells[-2] = [half_before(e, True) for e in cells[2]]
    cells[-1] = [half_before(e, True) for e in cells[3]]
    cells[4] = [half_after(e, True) for e in cells[0]]
    cells[5] = [half_after(e, True) for e in cells[1]]
    from_before, from_after, along_x, tables = {}, {}, {}, {}
    for t in range(-2, 5):
        table, velocity, pressure = jacobian_entries(cells[t])
        tables[t] = [[None if e is None else SCALE * e for e in x] for x in table]
        from_before[t] = scaled_plus(table, SCALE, SHARE)
        from_after[t] = scaled_plus(table, -SCALE, SHARE)
        along_x[t] = flux_along(cells[t], velocity, pressure, 0)
    from_before[-1] = kept_where(jnp.logical_not(first_half), from_before[-1])
    from_after[4] = kept_where(jnp.logical_not(last_half), from_after[4])
    right = {}
    for t in range(4):
        right[t] = []
        for c in range(5):
            fourth = (
                (cells[t + 2][c] + cells[t - 2][c])
                - 4.0 * (cells[t + 1][c] + cells[t - 1][c])
                + 6.0 * cells[t][c]
            )
            total = partial[c][t] - SPEED * (along_x[t + 1][c] - along_x[t - 1][c]) - DAMP * fourth
            right[t].append([total * SHARE])
    right[-1] = mapped(half_before, right[3])

    def eliminated(t):
        if t == 2:
            outer, inner = tables[t + 1], tables[t - 1]
            matrix = multiply(add_tables(outer, inner), tables[t])
            for i in range(5):
                for j in range(5):
                    if outer[i][j] is not None:
                        change = SHARE * (outer[i][j] - inner[i][j])
                        matrix[i][j] = change if matrix[i][j] is None else matrix[i][j] + change
                matrix[i][i] = matrix[i][i] + (1.0 - 2.0 * SHARE * SHARE)
        else:
            matrix = identity_minus(
                add_tables(
                    multiply(from_after[t + 1], from_before[t]),
                    multiply(from_before[t - 1], from_after[t]),
                )
            )
        before = dense(multiply(from_before[t - 1], from_before[t - 2]))
        after = dense(multiply(from_after[t + 1], from_after[t + 2]))
        value = add_tables(
            right[t],
            add_tables(
                multiply(from_after[t + 1], right[t + 1]), multiply(from_before[t - 1], right[t - 1])
            ),
        )
        return matrix, before, after, value

    matrix, before, after, value = eliminated(2)
    solved = solve(matrix, side_by_side(before, after, value))
    fine_before, fine_after, fine_value = (
        columns_of(solved, 0, 5), columns_of(solved, 5, 10), columns_of(solved, 10, 11)
    )
    matrix, before, after, value = eliminated(0)
    matrix = minus(
        matrix,
        add_tables(
            multiply(after, fine_before), multiply(before, mapped(half_before, fine_after))
        ),
    )
    value = add_tables(
        value,
        add_tables(multiply(after, fine_value), multiply(before, mapped(half_before, fine_value))),
    )
    before = multiply(before, mapped(half_before, fine_before))
    after = multiply(after, fine_after)

    def pick(table, function):
        return mapped(lambda e: function(e, swapped_halves(e)), table)

    packed = [[in_top(a, swapped_halves(b)) for a, b in zip(x, y)] for x, y in zip(before, after)]
    second = [[in_top(swapped_halves(a), b) for a, b in zip(x, y)] for x, y in zip(before, after)]
    second_matrix = pick(matrix, lambda e, swapped: in_top(swapped, e))
    second_value = pick(value, lambda e, swapped: in_top(swapped, e))
    matrix = pick(matrix, in_top)
    value = pick(value, in_top)
    solved = solve(second_matrix, side_by_side(second, second_value))
    second, second_value = columns_of(solved, 0, 5), columns_of(solved, 5, 6)

    def top_before(table):
        return mapped(lambda e: in_top(blocks_before(e, 1), e), table)

    matrix = minus(matrix, both_halves(multiply(packed, mapped(half_before, second))))
    value = add_tables(value, both_halves(multiply(packed, top_before(second_value))))
    packed = multiply(packed, top_before(second))
    solved = solve(matrix, side_by_side(packed, value))
    packed, value = columns_of(solved, 0, 5), columns_of(solved, 5, 6)

    stride = 1
    while stride < 16:
        earlier = lambda table: mapped(lambda e: blocks_before(e, stride), table)
        later = lambda table: mapped(lambda e: blocks_after(e, stride), table)
        towards = lambda x, y: [[in_top(a, b) for a, b in zip(p, q)] for p, q in zip(x, y)]
        prior, following = earlier(packed), later(packed)
        crossed = mapped(swapped_halves, towards(following, prior))
        matrix = minus_identity(both_halves(multiply(packed, crossed)))
        beside = towards(earlier(value), later(value))
        moved = both_halves(multiply(packed, beside))
        value = add_tables(moved, value) if stride == 1 else minus(moved, value)
        packed = multiply(packed, towards(prior, following))
        solved = solve(matrix, side_by_side(packed, value))
        packed, value = columns_of(solved, 0, 5), columns_of(solved, 5, 6)
        stride *= 2

    other_half = (row < 4) == ((row & 3) < 2)
    only = mapped(lambda e: jnp.where(other_half, swapped_halves(e), e), packed)
    partner = lambda table: mapped(lambda e: roll_rows(e, 2), table)
    matrix = minus_identity(multiply(only, partner(only)))
    value = solve(matrix, minus(multiply(only, partner(value)), value))
    value = mapped(lambda e: -e, value)
    last_block = ((row & 3) == 3) & (lane >= 112)
    ahead = mapped(lambda e: jnp.where(last_block, 0.0, blocks_after(e, 1)), value)
    around = [[in_top(a[0], b[0])] for a, b in zip(value, ahead)]
    middle = add_tables(second_value, both_halves(multiply(second, around)))
    result = {
        0: [[in_top(a[0], b[0])] for a, b in zip(value, middle)],
        4: [[in_top(a[0], b[0])] for a, b in zip(middle, ahead)],
    }
    result[2] = add_tables(
        fine_value, add_tables(multiply(fine_before, result[0]), multiply(fine_after, result[4]))
    )
    for t in (1, 3):
        result[t] = add_tables(
            right[t],
            add_tables(
                multiply(from_before[t - 1], result[t - 1]), multiply(from_after[t + 1], result[t + 1])
            ),
        )
    for c in range(5):
        tiles = swap_bit(swap_bit([result[t][c][0] for t in range(4)], 2, 32), 1, 16)
        for u in range(4):
            tile = exchanged(tiles[u])
            for j in range(2):
                out_ref[pl.ds((u + 4 * j) * 5 + c, 4, stride=40), :] = tile[4 * j : 4 * j + 4]


def unpack_kernel(returned_ref, out_ref):
    for c in range(5):
        tiles = [returned_ref[pl.ds(g * 5 + c, 4, stride=40), :] for g in range(8)]
        tiles = swap_bit(tiles, 4, 64)
        tiles = swap_bit(tiles, 2, 32)
        tiles = swap_bit(tiles, 1, 16)
        for x in range(8):
            out_ref[c * 32 + x * 4 : c * 32 + x * 4 + 4, :] = tiles[x]


def call(kernel, rows, *operands, **options):
    whole = pl.BlockSpec(memory_space=pltpu.VMEM)
    return pl.pallas_call(
        kernel,
        out_shape=jax.ShapeDtypeStruct((rows, 128), jnp.float32),
        in_specs=[whole] * len(operands),
        out_specs=whole,
        compiler_params=pltpu.CompilerParams(vmem_limit_bytes=32 * 1024 * 1024),
        **options,
    )(*operands)


def per_device(flow_state):
    flow = [flow_state[c].reshape(32, 128) for c in range(5)]
    count = lax.axis_size("gy")
    vmem = pl.BlockSpec(memory_space=pltpu.VMEM)
    edges = pl.pallas_call(
        edge_kernel,
        out_shape=[jax.ShapeDtypeStruct((20, 128), jnp.float32)] * 2,
        in_specs=[vmem] * 5,
        out_specs=[vmem] * 2,
        compiler_params=pltpu.CompilerParams(vmem_limit_bytes=32 * 1024 * 1024),
    )(*flow)
    exchanges = [None, None]
    for start in (1, 0):
        pairs = [((start + i) % count, (start + i + 1) % count) for i in range(0, count, 2)]
        exchanges[start] = lax.ppermute(edges[start], "gy", pairs + [(b, a) for a, b in pairs])
    cost = pl.CostEstimate(flops=4000000, bytes_accessed=250000, transcendentals=0)
    packed = call(pack_kernel, 320, *flow, cost_estimate=cost)
    packed = call(border_kernel, 320, packed, *exchanges, input_output_aliases={0: 0})
    received = lax.all_to_all(
        packed.reshape(32, 1, 1280), "gx", split_axis=0, concat_axis=0, tiled=True
    ).reshape(320, 128)
    solved = call(line_kernel, 160, received)
    returned = lax.all_to_all(
        solved.reshape(32, 1, 640), "gx", split_axis=0, concat_axis=0, tiled=True
    ).reshape(160, 128)
    return call(unpack_kernel, 160, returned).reshape(flow_state.shape)


def solution(mesh):
    placed = (P(None, "gx", None, "gy"),)
    return jax.shard_map(
        per_device, mesh=mesh, in_specs=placed, out_specs=P(None, "gx", None, "gy"), check_vma=False
    )
```
